32 devices in a mesh: row: 8 (over y, x, core), col: 4 (over z).
Axes of the slice: x: 2, y: 2, z: 4, core: 2. Of those that a mesh axis runs over, the one named last changes fastest.
Arguments:
- field: bfloat16 [8, 1536, 2, 2, 512], P(None, 'row', None, None, 'col'), may hold values from -6 to 6
- coef: float32 [1536, 512], P('row', 'col'), may hold values from 0.3 to 3
- table: bfloat16 [8, 1024, 1536], P('row'), may hold values from -0.15625 to 0.15625
- order_ids: int32 [8], P('row'), may hold values from 0 to 1023, as said below
- inverses: bfloat16 [1024, 512, 512], P(('row', 'col')), may hold values from -0.25 to 0.25
- degree_owner: int32 [1024], replicated, may hold values from 0 to 1023, each once
Outputs:
- synthesized: bfloat16 [8, 1536, 2, 2, 512], P(None, 'row', None, None, 'col')
The draws below stay inside these ranges and needn't reach their ends.
Inputs may be any that keep to these rules, and one draw needn't show every extreme that they name: `order_ids`: distinct orders; 0 and 1023 are always among them. `degree_owner`: every degree appears exactly once.
All inputs are finite; a program needn't handle non-finite values.
Results may differ from the reference program's by a relative error of at most 0.0064.
Values may be sent and summed in bfloat16 or wider, within the bound.
No kernel may reach another device: no remote copies, remote signals or barrier semaphores. Data moves between devices by JAX's collectives and lax.ppermute only.
A program may use at most 64 MiB of HBM per device.

```python
import math
import jax
import jax.numpy as jnp
from jax import lax

LDEG = 1024
LAT = 1536
RADII = 512
FIELDS = 2
ORDERS = 8


def draw_order_ids(key, part):
    first_key = jax.random.fold_in(key, 11)
    second_key = jax.random.fold_in(key, 23)
    middle = 1 + jax.random.permutation(first_key, LDEG - 2)[:ORDERS - 2]
    values = jnp.concatenate([jnp.array([0, LDEG - 1], jnp.int32), middle.astype(jnp.int32)])
    return values[jax.random.permutation(second_key, ORDERS)].astype(jnp.int32)


def block_levels(key, extent, split, low, top_value):
    level, own = 1.0, jax.random.fold_in(key, 6)
    for dim, blocks in split:
        draws = jnp.exp(jax.random.uniform(jax.random.fold_in(own, dim), (blocks,), jnp.float32, low / len(split), top_value / len(split)))
        level = level * jnp.repeat(draws, extent[dim] // blocks).reshape([-1 if axis == dim else 1 for axis in range(len(extent))])
    return level


def scatter_about(key, dims, width, most, pieces=(), kind=jnp.bfloat16):
    gain = block_levels(key, dims, pieces, -0.22, 0.18) if pieces else 1.0
    drawn = jax.random.normal(key, dims, jnp.float32) * width * gain
    return jnp.minimum(jnp.maximum(drawn, -most), most).astype(kind)


def setup_inputs(seed: int = 0) -> dict:
    streams_of = jax.random.split(jax.random.key(seed), 7)
    return {
        "field": scatter_about(streams_of[0], (ORDERS, LAT, FIELDS, 2, RADII), 1.0, 6.0, ((1, 8), (4, 4))),
        "coef": jnp.clip(jnp.exp(math.log(3.0) - 2.3025851 * jax.random.uniform(streams_of[1], (LAT, RADII), jnp.float32) ** block_levels(streams_of[1], (LAT, RADII), ((0, 8), (1, 4)), -0.2, 0.2)), 0.3, 3.0),
        "table": scatter_about(streams_of[2], (ORDERS, LDEG, LAT), LAT ** -0.5, 0.15625, ((0, 8),)),
        "order_ids": draw_order_ids(jax.random.fold_in(streams_of[6], 71), 0),
        "inverses": scatter_about(streams_of[4], (LDEG, RADII, RADII), RADII ** -0.5, 0.25, ((0, 32),)),
        "degree_owner": jax.random.permutation(streams_of[5], LDEG).astype(jnp.int32),
    }


def reference(field, coef, table, order_ids, inverses, degree_owner):
    weighted = (field.astype(jnp.float32) * coef[None, :, None, None, :]).astype(jnp.bfloat16)
    degrees = lax.iota(jnp.int32, LDEG)

    def analyze(inputs):
        table_rows, columns, order_id = inputs
        product = jnp.dot(table_rows, columns.reshape(LAT, FIELDS * 2 * RADII), preferred_element_type=jnp.float32)
        product = jnp.where((degrees >= order_id)[:, None], product, 0.0)
        return product.astype(jnp.bfloat16).reshape(LDEG, FIELDS, 2, RADII)

    spectral = lax.map(analyze, (table, weighted, order_ids))
    placed = jnp.take(spectral, degree_owner, axis=1)
    solved_placed = jnp.einsum("kpfcs,prs->kpfcr", placed.astype(jnp.float32), inverses.astype(jnp.float32)).astype(jnp.bfloat16)
    inverse_order = jnp.zeros((LDEG,), jnp.int32).at[degree_owner].set(degrees)
    solved = jnp.take(solved_placed, inverse_order, axis=1)

    def synthesize(inputs):
        table_rows, coeffs = inputs
        product = jnp.dot(table_rows.T, coeffs.reshape(LDEG, FIELDS * 2 * RADII), preferred_element_type=jnp.float32)
        return product.astype(jnp.bfloat16).reshape(LAT, FIELDS, 2, RADII)

    return lax.map(synthesize, (table, solved))
```

```python
import functools

import jax
import jax.numpy as jnp
from jax import lax
from jax.experimental import pallas as pl
from jax.experimental.pallas import tpu as pltpu
from jax.sharding import PartitionSpec as P

LANES = 128
SUBLANES = 8


def solve_kernel(orders, shards, members, x_ref, inv_ref, y_ref, x32, y32):
    step = pl.program_id(0)
    per_step = inv_ref.shape[0]
    degrees = x_ref.shape[0] // (orders * shards)

    @pl.when(step == 0)
    def _():
        for m in range(members):
            x32[m] = x_ref[:, m * LANES : (m + 1) * LANES].astype(jnp.float32)

    for local in range(per_step):
        degree = step * per_step + local

        def rows(shard):
            return pl.ds(shard * degrees + degree, orders, stride=shards * degrees)

        x = jnp.concatenate(
            [
                jnp.concatenate([x32[m, rows(r), :] for r in range(shards)], axis=1)
                for m in range(members)
            ],
            axis=0,
        ).astype(jnp.bfloat16)
        y = lax.dot_general(
            x, inv_ref[local], (((1,), (1,)), ((), ())), preferred_element_type=jnp.float32
        )
        for m in range(members):
            for r in range(shards):
                y32[m, rows(r), :] = y[
                    m * orders : (m + 1) * orders, r * LANES : (r + 1) * LANES
                ]

    @pl.when(step == pl.num_programs(0) - 1)
    def _():
        for m in range(members):
            y_ref[:, m * LANES : (m + 1) * LANES] = y32[m].astype(jnp.bfloat16)


def solve(owned, inverses, orders, shards, members):
    blocks, degrees, columns = owned.shape
    radii = inverses.shape[1]
    if columns != members * LANES or orders != SUBLANES or degrees % 4:
        split = owned.reshape(orders, shards, degrees, members, radii // shards)
        solved = jnp.einsum(
            "kadms,dtas->kdmt",
            split,
            inverses.reshape(degrees, radii, shards, radii // shards),
            preferred_element_type=jnp.float32,
        ).astype(jnp.bfloat16)
        solved = solved.reshape(orders, degrees, members, shards, radii // shards)
        return solved.transpose(0, 3, 1, 2, 4).reshape(owned.shape)
    per_step = 4
    rows = blocks * degrees
    out = pl.pallas_call(
        functools.partial(solve_kernel, orders, shards, members),
        grid=(degrees // per_step,),
        out_shape=jax.ShapeDtypeStruct((rows, columns), jnp.bfloat16),
        in_specs=[
            pl.BlockSpec((rows, columns), lambda i: (0, 0)),
            pl.BlockSpec((per_step, radii, radii), lambda i: (i, 0, 0)),
        ],
        out_specs=pl.BlockSpec((rows, columns), lambda i: (0, 0)),
        scratch_shapes=[
            pltpu.VMEM((members, rows, LANES), jnp.float32),
            pltpu.VMEM((members, rows, LANES), jnp.float32),
        ],
        compiler_params=pltpu.CompilerParams(vmem_limit_bytes=40 * 1024 * 1024),
        cost_estimate=pl.CostEstimate(
            flops=2 * degrees * radii * radii * orders * members,
            bytes_accessed=inverses.size * 2 + 4 * rows * columns,
            transcendentals=0,
        ),
    )(owned.reshape(rows, columns), inverses)
    return out.reshape(owned.shape)


def per_device(field, coef, table, order_ids, inverses, degree_owner):
    both = ("row", "col")
    n_row = lax.axis_size("row")
    n_col = lax.axis_size("col")
    orders, latitudes_dev = field.shape[:2]
    members = field.shape[2] * field.shape[3]
    columns = members * field.shape[4]
    ord_dev, degrees_all, latitudes = table.shape
    deg_dev = inverses.shape[0]
    devices = n_row * n_col

    weighted = (field.astype(jnp.float32) * coef[None, :, None, None, :]).astype(jnp.bfloat16)
    weighted = weighted.reshape(n_row, ord_dev, latitudes_dev, columns)
    arrived = lax.all_to_all(weighted, "row", split_axis=0, concat_axis=0, tiled=True)
    arrived = arrived.swapaxes(0, 1).reshape(ord_dev, latitudes, columns)

    degrees = lax.iota(jnp.int32, degrees_all)
    chosen = (degree_owner[:, None] == degrees[None, :])[None] & (
        degrees[None, None, :] >= order_ids[:, None, None]
    )
    chosen = chosen.astype(jnp.bfloat16)
    placed_table = jnp.einsum(
        "kpl,klt->kpt", chosen, table, preferred_element_type=jnp.float32
    ).astype(jnp.bfloat16)
    turned_table = jnp.einsum(
        "klt,kpl->ktp", table, chosen, preferred_element_type=jnp.float32
    ).astype(jnp.bfloat16)

    spectral = jnp.einsum(
        "kpt,ktn->kpn", placed_table, arrived, preferred_element_type=jnp.float32
    ).astype(jnp.bfloat16)
    spectral = spectral.reshape(ord_dev, devices, deg_dev, columns).swapaxes(0, 1)
    owned = lax.all_to_all(spectral, both, split_axis=0, concat_axis=0, tiled=True)
    owned = owned.reshape(n_row, n_col, ord_dev, deg_dev, columns).swapaxes(1, 2)
    solved = solve(
        owned.reshape(orders * n_col, deg_dev, columns), inverses, orders, n_col, members
    )
    solved = solved.reshape(n_row, ord_dev, n_col, deg_dev, columns).swapaxes(1, 2)
    solved = solved.reshape(devices, ord_dev, deg_dev, columns)
    coeffs = lax.all_to_all(solved, both, split_axis=0, concat_axis=0, tiled=True)
    coeffs = coeffs.swapaxes(0, 1).reshape(ord_dev, degrees_all, columns)
    outputs = jnp.einsum(
        "ktp,kpn->ktn", turned_table, coeffs, preferred_element_type=jnp.float32
    ).astype(jnp.bfloat16)
    outputs = outputs.reshape(ord_dev, n_row, latitudes_dev, columns).swapaxes(0, 1)
    outputs = lax.all_to_all(outputs, "row", split_axis=0, concat_axis=0, tiled=True)
    return outputs.reshape(field.shape)


def solution(mesh):
    in_specs = (
        P(None, "row", None, None, "col"),
        P("row", "col"),
        P("row", None, None),
        P("row"),
        P(("row", "col"), None, None),
        P(),
    )
    out_specs = P(None, "row", None, None, "col")
    return jax.shard_map(
        per_device, mesh=mesh, in_specs=in_specs, out_specs=out_specs, check_vma=False
    )
```

```python
import functools

import jax
import jax.numpy as jnp
from jax import lax
from jax.experimental import pallas as pl
from jax.experimental.pallas import tpu as pltpu
from jax.sharding import PartitionSpec as P

LANES = 128
SUBLANES = 8
UNROLL = 4
PREPARE_FLOPS = 5 * 10**9
MIB = 1024 * 1024
BF16 = jnp.bfloat16
F32 = jnp.float32
VMEM = pl.BlockSpec(memory_space=pltpu.VMEM)
SMEM = pl.BlockSpec(memory_space=pltpu.SMEM)
HBM = pl.BlockSpec(memory_space=pltpu.HBM)
ANY = pl.BlockSpec(memory_space=pl.ANY)


def dot(a, b):
    return jnp.dot(a, b, preferred_element_type=F32)


def params(mib):
    return pltpu.CompilerParams(vmem_limit_bytes=mib * MIB)


def in_hbm(array):
    return pltpu.with_memory_space_constraint(array, pltpu.HBM)


def cost(flops, moved):
    return pl.CostEstimate(flops=flops, bytes_accessed=moved, transcendentals=0)


def start(*copies):
    for copy in copies:
        copy.start()


def wait(*copies):
    for copy in copies:
        copy.wait()


def tiles(rows, count):
    return [pl.ds(i * (rows // count), rows // count) for i in range(count)]


def fetches(source, target, sems):
    parts = tiles(source.shape[0], sems.shape[0])
    copies = [
        pltpu.make_async_copy(source.at[part], target.at[part], sems.at[i])
        for i, part in enumerate(parts)
    ]
    return list(zip(parts, copies))


def weigh_kernel(members, x_hbm, coef_hbm, out_hbm, x16, x32, y16, coef, coef_sem, in_sems, out_sems):
    orders = in_sems.shape[0]
    lats = coef.shape[0]
    coef_copy = pltpu.make_async_copy(coef_hbm, coef, coef_sem)
    coef_copy.start()
    parts = fetches(x_hbm, x16, in_sems)
    start(*[copy for _, copy in parts])
    coef_copy.wait()
    stores = []
    for k, (rows, copy) in enumerate(parts):
        copy.wait()
        slot = k % 2
        x32[slot] = x16[rows, :].astype(F32)
        for m in range(members):
            part = x32[slot, pl.ds(m, lats, stride=members), :]
            y16[k, :, m * LANES : (m + 1) * LANES] = (part * coef[...]).astype(BF16)
        stores.append(pltpu.make_async_copy(y16.at[k], out_hbm.at[k], out_sems.at[k]))
        stores[-1].start()
    wait(*stores)


def weigh(field, coef):
    orders, lats, groups, parts, _ = field.shape
    members = groups * parts
    block = lats * members
    shape = (orders, lats, members * LANES)
    return pl.pallas_call(
        functools.partial(weigh_kernel, members),
        out_shape=pltpu.HBM(shape, BF16),
        in_specs=[HBM, HBM],
        out_specs=HBM,
        scratch_shapes=[
            pltpu.VMEM((orders * block, LANES), BF16),
            pltpu.VMEM((2, block, LANES), F32),
            pltpu.VMEM(shape, BF16),
            pltpu.VMEM(coef.shape, F32),
            pltpu.SemaphoreType.DMA,
            pltpu.SemaphoreType.DMA((orders,)),
            pltpu.SemaphoreType.DMA((orders,)),
        ],
        compiler_params=params(16),
        cost_estimate=cost(field.size, field.size * 4),
    )(in_hbm(field.reshape(orders * block, LANES)), in_hbm(coef))


def analyse_kernel(table_hbm, chosen_hbm, fields, out_ref, w, s, table, chosen, sems, table_sems, chosen_sems):
    field_parts = fetches(fields, w, sems)
    start(*[copy for _, copy in field_parts])
    table_parts = fetches(table_hbm, table, table_sems)
    start(*[copy for _, copy in table_parts])
    chosen_parts = fetches(chosen_hbm, chosen, chosen_sems)
    start(*[copy for _, copy in chosen_parts])
    wait(*[copy for _, copy in field_parts])
    for rows, copy in table_parts:
        copy.wait()
        s[rows, :] = dot(table[rows, :], w[...]).astype(BF16)
    for rows, copy in chosen_parts:
        copy.wait()
        out_ref[rows, :] = dot(chosen[rows, :], s[...]).astype(BF16)


def analyse(table, chosen, fields):
    rows, lats = table.shape
    columns = fields.shape[1]
    return pl.pallas_call(
        analyse_kernel,
        out_shape=jax.ShapeDtypeStruct((rows, columns), BF16),
        in_specs=[HBM, HBM, ANY],
        out_specs=VMEM,
        scratch_shapes=[
            pltpu.VMEM((lats, columns), BF16),
            pltpu.VMEM((rows, columns), BF16),
            pltpu.VMEM(table.shape, BF16),
            pltpu.VMEM(chosen.shape, BF16),
            pltpu.SemaphoreType.DMA((8,)),
            pltpu.SemaphoreType.DMA((4,)),
            pltpu.SemaphoreType.DMA((4,)),
        ],
        compiler_params=params(20),
        cost_estimate=cost(2 * rows * (lats + rows) * columns, 2 * rows * (lats + rows)),
    )(in_hbm(table), in_hbm(chosen), fields)


def prepare_kernel(order_ref, table_hbm, owner_ref, *rest):
    turned_hbm, chosen_hbm, back_hbm, table, turned, chosen, back, table_sem, sems = rest
    table_copy = pltpu.make_async_copy(table_hbm, table, table_sem)
    table_copy.start()
    degrees, lats = table.shape
    order = order_ref[0]
    owner = jnp.broadcast_to(owner_ref[...], (LANES, degrees))
    across = owner.T
    for block in range(degrees // LANES):
        part = slice(block * LANES, (block + 1) * LANES)
        degree = lax.broadcasted_iota(jnp.int32, (degrees, LANES), 1) + block * LANES
        chosen[:, part] = ((across == degree) & (degree >= order)).astype(F32).astype(BF16)
        degree = lax.broadcasted_iota(jnp.int32, (LANES, degrees), 0) + block * LANES
        back[part, :] = ((owner == degree) & (degree >= order)).astype(F32).astype(BF16)
    chosen_copy = pltpu.make_async_copy(chosen, chosen_hbm, sems.at[0])
    back_copy = pltpu.make_async_copy(back, back_hbm, sems.at[1])
    start(chosen_copy, back_copy)
    table_copy.wait()

    @pl.loop(0, lats // LANES)
    def _(i):
        part = pl.ds(pl.multiple_of(i * LANES, LANES), LANES)
        turned[part, :] = table[:, part].T

    turned_copy = pltpu.make_async_copy(turned, turned_hbm, sems.at[2])
    turned_copy.start()
    wait(chosen_copy, back_copy, turned_copy)


def prepare(order_ids, table, degree_owner):
    degrees, lats = table.shape
    shapes = [(lats, degrees), (degrees, degrees), (degrees, degrees)]
    return pl.pallas_call(
        prepare_kernel,
        out_shape=[pltpu.HBM(shape, BF16) for shape in shapes],
        in_specs=[SMEM, HBM, VMEM],
        out_specs=[HBM] * 3,
        scratch_shapes=[pltpu.VMEM(shape, BF16) for shape in [table.shape] + shapes]
        + [pltpu.SemaphoreType.DMA, pltpu.SemaphoreType.DMA((3,))],
        compiler_params=params(20),
        cost_estimate=cost(PREPARE_FLOPS, 4 * table.size),
    )(order_ids, in_hbm(table), degree_owner.reshape(1, degrees))


def solve_kernel(orders, shards, members, x_ref, inv_hbm, y_ref, x32, y32, inv, sems):
    degrees = inv.shape[0]
    chunks = sems.shape[0]
    parts = fetches(inv_hbm, inv, sems)
    start(*[copy for _, copy in parts])
    for m in range(members):
        x32[m] = x_ref[:, m * LANES : (m + 1) * LANES].astype(F32)

    @pl.loop(0, chunks)
    def _(i):
        each = degrees // chunks
        rows = pl.ds(i * each, each)
        pltpu.make_async_copy(inv_hbm.at[rows], inv.at[rows], sems.at[i]).wait()
        for local in range(each):
            degree = i * each + local

            def rows(shard):
                return pl.ds(shard * degrees + degree, orders, stride=shards * degrees)

            x = jnp.concatenate(
                [
                    jnp.concatenate([x32[m, rows(r), :] for r in range(shards)], axis=1)
                    for m in range(members)
                ],
                axis=0,
            ).astype(BF16)
            y = lax.dot_general(
                x, inv[degree], (((1,), (1,)), ((), ())), preferred_element_type=F32
            )
            for m in range(members):
                for r in range(shards):
                    y32[m, rows(r), :] = y[
                        m * orders : (m + 1) * orders, r * LANES : (r + 1) * LANES
                    ]

    for m in range(members):
        y_ref[:, m * LANES : (m + 1) * LANES] = y32[m].astype(BF16)


def solve(owned, inverses, orders, shards, members):
    rows, columns = owned.shape
    degrees, radii, _ = inverses.shape
    return pl.pallas_call(
        functools.partial(solve_kernel, orders, shards, members),
        out_shape=jax.ShapeDtypeStruct((rows, columns), BF16),
        in_specs=[VMEM, HBM],
        out_specs=VMEM,
        scratch_shapes=[pltpu.VMEM((members, rows, LANES), F32)] * 2
        + [pltpu.VMEM(inverses.shape, BF16), pltpu.SemaphoreType.DMA((degrees // UNROLL,))],
        compiler_params=params(30),
        cost_estimate=cost(2 * degrees * radii * radii * orders * members, 2 * inverses.size),
    )(owned, in_hbm(inverses))


def synthesise_kernel(turned_ref, back_ref, coeffs_ref, out_hbm, s, y, sems):
    for rows in tiles(back_ref.shape[0], 4):
        s[rows, :] = dot(back_ref[rows, :], coeffs_ref[...]).astype(BF16)
    copies = []
    for i, rows in enumerate(tiles(turned_ref.shape[0], sems.shape[0])):
        y[rows, :] = dot(turned_ref[rows, :], s[...]).astype(BF16)
        copies.append(pltpu.make_async_copy(y.at[rows], out_hbm.at[rows], sems.at[i]))
        copies[-1].start()
    wait(*copies)


def synthesise(turned, back, coeffs):
    lats, degrees = turned.shape
    columns = coeffs.shape[1]
    return pl.pallas_call(
        synthesise_kernel,
        out_shape=pltpu.HBM((lats, columns), BF16),
        in_specs=[VMEM] * 3,
        out_specs=HBM,
        scratch_shapes=[
            pltpu.VMEM((degrees, columns), BF16),
            pltpu.VMEM((lats, columns), BF16),
            pltpu.SemaphoreType.DMA((6,)),
        ],
        compiler_params=params(16),
        cost_estimate=cost(
            2 * degrees * (lats + degrees) * columns, 2 * degrees * (lats + degrees)
        ),
    )(turned, back, coeffs)


def assemble_kernel(members, x_any, out_hbm, x16, y32, y16, in_sems, out_sems):
    orders, lats = x16.shape[:2]
    block = lats * members
    parts = fetches(x_any, x16, in_sems)
    start(*[copy for _, copy in parts])
    copies = []
    for k, (_, copy) in enumerate(parts):
        copy.wait()
        slot = k % 2
        for m in range(members):
            part = x16[k, :, m * LANES : (m + 1) * LANES].astype(F32)
            y32[slot, pl.ds(m, lats, stride=members), :] = part
        rows = pl.ds(k * block, block)
        y16[rows, :] = y32[slot].astype(BF16)
        copies.append(pltpu.make_async_copy(y16.at[rows], out_hbm.at[rows], out_sems.at[k]))
        copies[-1].start()
    wait(*copies)


def assemble(received, shape):
    orders, lats, groups, parts, _ = shape
    members = groups * parts
    block = lats * members
    out = pl.pallas_call(
        functools.partial(assemble_kernel, members),
        out_shape=pltpu.HBM((orders * block, LANES), BF16),
        in_specs=[ANY],
        out_specs=HBM,
        scratch_shapes=[
            pltpu.VMEM(received.shape, BF16),
            pltpu.VMEM((2, block, LANES), F32),
            pltpu.VMEM((orders * block, LANES), BF16),
            pltpu.SemaphoreType.DMA((orders,)),
            pltpu.SemaphoreType.DMA((orders,)),
        ],
        compiler_params=params(16),
        cost_estimate=cost(orders * block * LANES, orders * block * LANES * 4),
    )(received)
    return out.reshape(shape)


def exchange_rows(blocks):
    return lax.all_to_all(blocks, "row", split_axis=0, concat_axis=0, tiled=True)


def exchange_degrees(blocks):
    return lax.all_to_all(blocks, ("row", "col"), split_axis=0, concat_axis=0, tiled=True)


def tiled(field, coef, table, order_ids, inverses, degree_owner):
    n_row = lax.axis_size("row")
    n_col = lax.axis_size("col")
    orders, lats_dev, groups, parts, radii_dev = field.shape
    degrees_all, lats = table.shape[1:]
    deg_dev = inverses.shape[0]
    members = groups * parts
    columns = members * radii_dev

    weighted = weigh(field, coef)
    turned, chosen, back = prepare(order_ids, table[0], degree_owner)
    arrived = exchange_rows(weighted).reshape(lats, columns)
    spectral = analyse(table[0], chosen, arrived)
    owned = exchange_degrees(spectral.reshape(n_row * n_col, deg_dev, columns))
    solved = solve(owned.reshape(degrees_all, columns), inverses, orders, n_col, members)
    coeffs = exchange_degrees(solved.reshape(n_row * n_col, deg_dev, columns))
    outputs = synthesise(turned, back, coeffs.reshape(degrees_all, columns))
    received = exchange_rows(outputs.reshape(n_row, lats_dev, columns))
    return assemble(received, field.shape)


def general(field, coef, table, order_ids, inverses, degree_owner):
    both = ("row", "col")
    n_row = lax.axis_size("row")
    n_col = lax.axis_size("col")
    orders, latitudes_dev = field.shape[:2]
    members = field.shape[2] * field.shape[3]
    radii_dev = field.shape[4]
    columns = members * radii_dev
    ord_dev, degrees_all, latitudes = table.shape
    deg_dev, radii, _ = inverses.shape
    devices = n_row * n_col

    weighted = (field.astype(F32) * coef[None, :, None, None, :]).astype(BF16)
    weighted = weighted.reshape(n_row, ord_dev, latitudes_dev, columns)
    arrived = lax.all_to_all(weighted, "row", split_axis=0, concat_axis=0, tiled=True)
    arrived = arrived.swapaxes(0, 1).reshape(ord_dev, latitudes, columns)

    degrees = lax.iota(jnp.int32, degrees_all)
    chosen = (degree_owner[:, None] == degrees[None, :])[None] & (
        degrees[None, None, :] >= order_ids[:, None, None]
    )
    placed_table = jnp.einsum(
        "kpl,klt->kpt", chosen.astype(BF16), table, preferred_element_type=F32
    ).astype(BF16)
    spectral = jnp.einsum(
        "kpt,ktn->kpn", placed_table, arrived, preferred_element_type=F32
    ).astype(BF16)
    spectral = spectral.reshape(ord_dev, devices, deg_dev, columns).swapaxes(0, 1)
    owned = lax.all_to_all(spectral, both, split_axis=0, concat_axis=0, tiled=True)
    owned = owned.reshape(n_row, n_col, ord_dev, deg_dev, members, radii_dev).swapaxes(1, 2)
    owned = owned.reshape(orders, n_col, deg_dev, members, radii_dev)
    solved = jnp.einsum(
        "kadms,dtas->kdmt",
        owned,
        inverses.reshape(deg_dev, radii, n_col, radii_dev),
        preferred_element_type=F32,
    ).astype(BF16)
    solved = solved.reshape(n_row, ord_dev, deg_dev, members, n_col, radii_dev)
    solved = solved.transpose(0, 4, 1, 2, 3, 5).reshape(devices, ord_dev, deg_dev, columns)
    coeffs = lax.all_to_all(solved, both, split_axis=0, concat_axis=0, tiled=True)
    coeffs = coeffs.swapaxes(0, 1).reshape(ord_dev, degrees_all, columns)
    outputs = jnp.einsum(
        "kpt,kpn->ktn", placed_table, coeffs, preferred_element_type=F32
    ).astype(BF16)
    outputs = outputs.reshape(ord_dev, n_row, latitudes_dev, columns).swapaxes(0, 1)
    outputs = lax.all_to_all(outputs, "row", split_axis=0, concat_axis=0, tiled=True)
    return outputs.reshape(field.shape)


def per_device(field, coef, table, order_ids, inverses, degree_owner):
    orders, lats, _, _, radii_dev = field.shape
    n_row = lax.axis_size("row")
    fits = (
        orders == n_row == SUBLANES
        and radii_dev == LANES
        and lats % 16 == 0
        and inverses.shape[0] % 16 == 0
        and table.shape[1] % 256 == 0
    )
    form = tiled if fits else general
    return form(field, coef, table, order_ids, inverses, degree_owner)


def solution(mesh):
    in_specs = (
        P(None, "row", None, None, "col"),
        P("row", "col"),
        P("row", None, None),
        P("row"),
        P(("row", "col"), None, None),
        P(),
    )
    out_specs = P(None, "row", None, None, "col")
    return jax.shard_map(
        per_device, mesh=mesh, in_specs=in_specs, out_specs=out_specs, check_vma=False
    )
```

```python
import functools

import jax
import jax.numpy as jnp
from jax import lax
from jax.experimental import pallas as pl
from jax.experimental.pallas import tpu as pltpu
from jax.sharding import PartitionSpec as P

LANES = 128
SUBLANES = 8
HELD = 8
LATE = 6
PARTNERS = (0, 6, 2, 4, 7, 1, 3, 5)
MIB = 1024 * 1024
BF16 = jnp.bfloat16
F32 = jnp.float32
VMEM = pl.BlockSpec(memory_space=pltpu.VMEM)
SMEM = pl.BlockSpec(memory_space=pltpu.SMEM)
HBM = pl.BlockSpec(memory_space=pltpu.HBM)
ANY = pl.BlockSpec(memory_space=pl.ANY)


def dot(a, b):
    return jnp.dot(a, b, preferred_element_type=F32)


def params(mib):
    return pltpu.CompilerParams(vmem_limit_bytes=mib * MIB)


def in_hbm(array):
    return pltpu.with_memory_space_constraint(array, pltpu.HBM)


def cost(flops, moved):
    return pl.CostEstimate(flops=flops, bytes_accessed=moved, transcendentals=0)


def in_vmem(array):
    return pltpu.with_memory_space_constraint(array, pltpu.VMEM)


def start(*copies):
    for copy in copies:
        copy.start()


def wait(*copies):
    for copy in copies:
        copy.wait()


def tiles(rows, count):
    return [pl.ds(i * (rows // count), rows // count) for i in range(count)]


def fetches(source, target, sems):
    parts = tiles(source.shape[0], sems.shape[0])
    copies = [
        pltpu.make_async_copy(source.at[part], target.at[part], sems.at[i])
        for i, part in enumerate(parts)
    ]
    return list(zip(parts, copies))


def weigh_kernel(members, me_ref, x_hbm, coef_hbm, *rest):
    outs, (x16, x32, y16, coef, coef_sem, in_sems, out_sems) = rest[:-7], rest[-7:]
    lats = coef.shape[0]
    coef_copy = pltpu.make_async_copy(coef_hbm, coef, coef_sem)
    coef_copy.start()
    block = lats * members
    parts = []
    for j in range(len(outs)):
        rows = pl.ds(pl.multiple_of((me_ref[0] ^ PARTNERS[j]) * block, block), block)
        parts.append(pltpu.make_async_copy(x_hbm.at[rows], x16.at[j], in_sems.at[j]))
    start(*parts)
    coef_copy.wait()
    stores = []
    for j, copy in enumerate(parts):
        copy.wait()
        slot = j % 2
        x32[slot] = x16[j].astype(F32)
        for m in range(members):
            part = x32[slot, pl.ds(m, lats, stride=members), :]
            y16[j, :, m * LANES : (m + 1) * LANES] = (part * coef[...]).astype(BF16)
        stores.append(pltpu.make_async_copy(y16.at[j], outs[j], out_sems.at[j]))
        stores[-1].start()
    wait(*stores)


def weigh(me, field, coef):
    orders, lats, groups, parts, _ = field.shape
    members = groups * parts
    block = lats * members
    shape = (orders, lats, members * LANES)
    return pl.pallas_call(
        functools.partial(weigh_kernel, members),
        out_shape=[pltpu.HBM(shape[1:], BF16)] * orders,
        in_specs=[SMEM, HBM, HBM],
        out_specs=[HBM] * orders,
        scratch_shapes=[
            pltpu.VMEM((orders, block, LANES), BF16),
            pltpu.VMEM((2, block, LANES), F32),
            pltpu.VMEM(shape, BF16),
            pltpu.VMEM(coef.shape, F32),
            pltpu.SemaphoreType.DMA,
            pltpu.SemaphoreType.DMA((orders,)),
            pltpu.SemaphoreType.DMA((orders,)),
        ],
        compiler_params=params(16),
        cost_estimate=cost(field.size, field.size * 4),
    )(me, in_hbm(field.reshape(orders * block, LANES)), in_hbm(coef))


def analyse_kernel(me_ref, table_ref, inv_hbm, *rest):
    blocks, (out_ref, inv_ref, w, inv_sem) = rest[:-4], rest[-4:]
    inv_copy = pltpu.make_async_copy(inv_hbm.at[: inv_ref.shape[0]], inv_ref, inv_sem)
    inv_copy.start()
    lats = blocks[0].shape[0]
    for j, block in enumerate(blocks):
        w[pl.ds(pl.multiple_of((me_ref[0] ^ PARTNERS[j]) * lats, lats), lats), :] = block[...]
    for rows in tiles(table_ref.shape[0], 4):
        out_ref[rows, :] = dot(table_ref[rows, :], w[...]).astype(BF16)
    inv_copy.wait()


def analyse(me, table, inverses, blocks):
    rows, lats = table.shape
    columns = blocks[0].shape[1]
    held = (inverses.shape[0] // HELD, *inverses.shape[1:])
    return pl.pallas_call(
        analyse_kernel,
        out_shape=[jax.ShapeDtypeStruct((rows, columns), BF16), pltpu.VMEM(held, BF16)],
        in_specs=[SMEM, VMEM, HBM] + [VMEM] * len(blocks),
        out_specs=[VMEM, VMEM],
        scratch_shapes=[pltpu.VMEM((lats, columns), BF16), pltpu.SemaphoreType.DMA],
        compiler_params=params(14),
        cost_estimate=cost(2 * rows * lats * columns, 2 * rows * lats + inverses.size),
    )(me, table, in_hbm(inverses), *blocks)


def place_kernel(order_ref, table_hbm, owner_hbm, placed_ref, table, owner, chosen, table_sem, owner_sem):
    owner_copy = pltpu.make_async_copy(owner_hbm, owner, owner_sem)
    table_copy = pltpu.make_async_copy(table_hbm, table, table_sem)
    start(owner_copy, table_copy)
    degrees = table.shape[0]
    order = order_ref[0]
    owner_copy.wait()
    across = jnp.broadcast_to(owner[...], (LANES, degrees)).T
    for block in range(degrees // LANES):
        part = slice(block * LANES, (block + 1) * LANES)
        degree = lax.broadcasted_iota(jnp.int32, (degrees, LANES), 1) + block * LANES
        chosen[:, part] = ((across == degree) & (degree >= order)).astype(F32).astype(BF16)
    table_copy.wait()
    for rows in tiles(degrees, 4):
        placed_ref[rows, :] = dot(chosen[rows, :], table[...]).astype(BF16)


def place(order_ids, table, degree_owner):
    degrees, lats = table.shape
    return pl.pallas_call(
        place_kernel,
        out_shape=jax.ShapeDtypeStruct((degrees, lats), BF16),
        in_specs=[SMEM, HBM, HBM],
        out_specs=VMEM,
        scratch_shapes=[
            pltpu.VMEM(table.shape, BF16),
            pltpu.VMEM((1, degrees), jnp.int32),
            pltpu.VMEM((degrees, degrees), BF16),
            pltpu.SemaphoreType.DMA,
            pltpu.SemaphoreType.DMA,
        ],
        compiler_params=params(16),
        cost_estimate=cost(2 * degrees * degrees * lats, 4 * table.size),
    )(order_ids, in_hbm(table), in_hbm(degree_owner.reshape(1, degrees)))


def turn_kernel(table_ref, turned_hbm, turned, sems):
    copies = []
    for i, rows in enumerate(tiles(turned.shape[0], 4)):
        turned[rows, :] = table_ref[:, rows.start : rows.start + rows.size].T
        copies.append(pltpu.make_async_copy(turned.at[rows], turned_hbm.at[rows], sems.at[i]))
        copies[-1].start()
    wait(*copies)


def turn(table):
    turned = table.shape[::-1]
    return pl.pallas_call(
        turn_kernel,
        out_shape=pltpu.HBM(turned, BF16),
        in_specs=[VMEM],
        out_specs=HBM,
        scratch_shapes=[pltpu.VMEM(turned, BF16), pltpu.SemaphoreType.DMA((4,))],
        compiler_params=params(12),
        cost_estimate=cost(table.size, 4 * table.size),
    )(table)


def solve_kernel(orders, shards, members, x_ref, here_ref, inv_hbm, y_ref, x32, y32, inv, sems):
    degrees, held = inv_hbm.shape[0], here_ref.shape[0]
    parts = fetches(inv_hbm.at[held:], inv, sems)
    start(*[copy for _, copy in parts])
    block = shards * degrees
    stride = x32.shape[1] // orders
    half = degrees // 2

    def widen(part):
        for k in range(orders):
            for r in range(shards):
                first = r * degrees + part * half
                rows, to = pl.ds(k * block + first, half), pl.ds(k * stride + first, half)
                for m in range(members):
                    x32[m, to, :] = x_ref[rows, m * LANES : (m + 1) * LANES].astype(F32)

    def narrow(part):
        for k in range(orders):
            for r in range(shards):
                first = r * degrees + part * half
                rows, at = pl.ds(k * block + first, half), pl.ds(k * stride + first, half)
                for m in range(members):
                    y_ref[rows, m * LANES : (m + 1) * LANES] = y32[m, at, :].astype(BF16)

    def apply(matrix, degree):
        def rows(shard):
            return pl.ds(shard * degrees + degree, orders, stride=stride)

        x = jnp.concatenate(
            [
                jnp.concatenate([x32[m, rows(r), :] for r in range(shards)], axis=1)
                for m in range(members)
            ],
            axis=0,
        ).astype(BF16)
        y = lax.dot_general(x, matrix, (((1,), (1,)), ((), ())), preferred_element_type=F32)
        for m in range(members):
            for r in range(shards):
                y32[m, rows(r), :] = y[m * orders : (m + 1) * orders, r * LANES : (r + 1) * LANES]

    each = (degrees - held) // len(parts)
    widen(0)
    for degree in range(degrees):
        if degree == half:
            widen(1)
            narrow(0)
        if degree < held:
            matrix = here_ref[degree]
        else:
            if (degree - held) % each == 0:
                parts[(degree - held) // each][1].wait()
            matrix = inv[degree - held]
        apply(matrix, degree)
    narrow(1)


def solve(owned, here, inverses, orders, shards, members):
    rows, columns = owned.shape
    degrees, radii, _ = inverses.shape
    rest = degrees - here.shape[0]
    return pl.pallas_call(
        functools.partial(solve_kernel, orders, shards, members),
        out_shape=jax.ShapeDtypeStruct((rows, columns), BF16),
        in_specs=[VMEM, VMEM, HBM],
        out_specs=VMEM,
        scratch_shapes=[pltpu.VMEM((members, rows + orders, LANES), F32)] * 2
        + [pltpu.VMEM((rest, radii, radii), BF16), pltpu.SemaphoreType.DMA((rest // 4,))],
        compiler_params=params(24),
        cost_estimate=cost(2 * degrees * radii * radii * orders * members, inverses.size),
    )(owned, in_vmem(here), in_hbm(inverses))


def synthesise_kernel(me_ref, turned_ref, coeffs_ref, *outs):
    lats = outs[0].shape[0]
    for j, out in enumerate(outs):
        rows = pl.ds(pl.multiple_of((me_ref[0] ^ PARTNERS[j]) * lats, lats), lats)
        out[...] = dot(turned_ref[rows, :], coeffs_ref[...]).astype(BF16)


def synthesise(me, turned, coeffs, partners):
    lats, degrees = turned.shape
    columns = coeffs.shape[1]
    return pl.pallas_call(
        synthesise_kernel,
        out_shape=[jax.ShapeDtypeStruct((lats // partners, columns), BF16)] * partners,
        in_specs=[SMEM] + [VMEM] * 2,
        out_specs=[VMEM] * partners,
        compiler_params=params(12),
        cost_estimate=cost(2 * degrees * lats * columns, 2 * degrees * lats),
    )(me, turned, coeffs)


def assemble_kernel(members, me_ref, *rest):
    blocks, (out_hbm, y32, y16, out_sems) = rest[:-4], rest[-4:]
    lats = blocks[0].shape[0]
    block = lats * members
    copies = []
    for j, x_ref in enumerate(blocks):
        slot = j % 2
        for m in range(members):
            part = x_ref[:, m * LANES : (m + 1) * LANES].astype(F32)
            y32[slot, pl.ds(m, lats, stride=members), :] = part
        y16[j] = y32[slot].astype(BF16)
        rows = pl.ds(pl.multiple_of((me_ref[0] ^ PARTNERS[j]) * block, block), block)
        copies.append(pltpu.make_async_copy(y16.at[j], out_hbm.at[rows], out_sems.at[j]))
        copies[-1].start()
    wait(*copies)


def assemble(me, received, shape):
    orders, lats, groups, parts, _ = shape
    members = groups * parts
    block = lats * members
    out = pl.pallas_call(
        functools.partial(assemble_kernel, members),
        out_shape=pltpu.HBM((orders * block, LANES), BF16),
        in_specs=[SMEM] + [VMEM] * orders,
        out_specs=HBM,
        scratch_shapes=[
            pltpu.VMEM((2, block, LANES), F32),
            pltpu.VMEM((orders, block, LANES), BF16),
            pltpu.SemaphoreType.DMA((orders,)),
        ],
        compiler_params=params(12),
        cost_estimate=cost(orders * block * LANES, orders * block * LANES * 4),
    )(me, *received)
    return out.reshape(shape)


def exchange_rows(blocks):
    n = lax.axis_size("row")
    return [
        block if not j else lax.ppermute(block, "row", [(a, a ^ j) for a in range(n)])
        for block, j in zip(blocks, PARTNERS)
    ]


def exchange_degrees(blocks):
    return lax.all_to_all(blocks, ("row", "col"), split_axis=0, concat_axis=0, tiled=True)


def tiled(field, coef, table, order_ids, inverses, degree_owner):
    n_row = lax.axis_size("row")
    n_col = lax.axis_size("col")
    orders, lats_dev, groups, parts, radii_dev = field.shape
    degrees_all, lats = table.shape[1:]
    deg_dev = inverses.shape[0]
    members = groups * parts
    columns = members * radii_dev

    me = lax.axis_index("row").astype(jnp.int32).reshape(1)

    weighted = list(weigh(me, field, coef))
    placed = place(order_ids, table[0], degree_owner)
    placed, *weighted[LATE:] = lax.optimization_barrier((placed, *weighted[LATE:]))
    arrived = exchange_rows(weighted)
    turned = turn(placed)
    turned, arrived[0] = lax.optimization_barrier((turned, arrived[0]))
    spectral, here = analyse(me, placed, inverses, arrived)
    owned = exchange_degrees(spectral.reshape(n_row * n_col, deg_dev, columns))
    solved = solve(owned.reshape(degrees_all, columns), here, inverses, orders, n_col, members)
    coeffs = exchange_degrees(solved.reshape(n_row * n_col, deg_dev, columns))
    outputs = synthesise(me, turned, coeffs.reshape(degrees_all, columns), n_row)
    return assemble(me, exchange_rows(outputs), field.shape)


def general(field, coef, table, order_ids, inverses, degree_owner):
    both = ("row", "col")
    n_row = lax.axis_size("row")
    n_col = lax.axis_size("col")
    orders, latitudes_dev = field.shape[:2]
    members = field.shape[2] * field.shape[3]
    radii_dev = field.shape[4]
    columns = members * radii_dev
    ord_dev, degrees_all, latitudes = table.shape
    deg_dev, radii, _ = inverses.shape
    devices = n_row * n_col

    weighted = (field.astype(F32) * coef[None, :, None, None, :]).astype(BF16)
    weighted = weighted.reshape(n_row, ord_dev, latitudes_dev, columns)
    arrived = lax.all_to_all(weighted, "row", split_axis=0, concat_axis=0, tiled=True)
    arrived = arrived.swapaxes(0, 1).reshape(ord_dev, latitudes, columns)

    degrees = lax.iota(jnp.int32, degrees_all)
    chosen = (degree_owner[:, None] == degrees[None, :])[None] & (
        degrees[None, None, :] >= order_ids[:, None, None]
    )
    placed_table = jnp.einsum(
        "kpl,klt->kpt", chosen.astype(BF16), table, preferred_element_type=F32
    ).astype(BF16)
    spectral = jnp.einsum(
        "kpt,ktn->kpn", placed_table, arrived, preferred_element_type=F32
    ).astype(BF16)
    spectral = spectral.reshape(ord_dev, devices, deg_dev, columns).swapaxes(0, 1)
    owned = lax.all_to_all(spectral, both, split_axis=0, concat_axis=0, tiled=True)
    owned = owned.reshape(n_row, n_col, ord_dev, deg_dev, members, radii_dev).swapaxes(1, 2)
    owned = owned.reshape(orders, n_col, deg_dev, members, radii_dev)
    solved = jnp.einsum(
        "kadms,dtas->kdmt",
        owned,
        inverses.reshape(deg_dev, radii, n_col, radii_dev),
        preferred_element_type=F32,
    ).astype(BF16)
    solved = solved.reshape(n_row, ord_dev, deg_dev, members, n_col, radii_dev)
    solved = solved.transpose(0, 4, 1, 2, 3, 5).reshape(devices, ord_dev, deg_dev, columns)
    coeffs = lax.all_to_all(solved, both, split_axis=0, concat_axis=0, tiled=True)
    coeffs = coeffs.swapaxes(0, 1).reshape(ord_dev, degrees_all, columns)
    outputs = jnp.einsum(
        "kpt,kpn->ktn", placed_table, coeffs, preferred_element_type=F32
    ).astype(BF16)
    outputs = outputs.reshape(ord_dev, n_row, latitudes_dev, columns).swapaxes(0, 1)
    outputs = lax.all_to_all(outputs, "row", split_axis=0, concat_axis=0, tiled=True)
    return outputs.reshape(field.shape)


def per_device(field, coef, table, order_ids, inverses, degree_owner):
    orders, lats, _, _, radii_dev = field.shape
    n_row = lax.axis_size("row")
    fits = (
        orders == n_row == SUBLANES
        and radii_dev == LANES
        and lats % 16 == 0
        and inverses.shape[0] % 16 == 0
        and table.shape[1] % 256 == 0
    )
    form = tiled if fits else general
    return form(field, coef, table, order_ids, inverses, degree_owner)


def solution(mesh):
    in_specs = (
        P(None, "row", None, None, "col"),
        P("row", "col"),
        P("row", None, None),
        P("row"),
        P(("row", "col"), None, None),
        P(),
    )
    out_specs = P(None, "row", None, None, "col")
    return jax.shard_map(
        per_device, mesh=mesh, in_specs=in_specs, out_specs=out_specs, check_vma=False
    )
```

```python
import functools

import jax
import jax.numpy as jnp
from jax import lax
from jax.experimental import pallas as pl
from jax.experimental.pallas import tpu as pltpu
from jax.sharding import PartitionSpec as P

LANES = 128
SUBLANES = 8
HELD = 24
RING = 12
FIRST = 5
LATE = 6
PARTNERS = (0, 6, 2, 4, 7, 1, 3, 5)
MIB = 1024 * 1024
BF16 = jnp.bfloat16
F32 = jnp.float32
VMEM = pl.BlockSpec(memory_space=pltpu.VMEM)
SMEM = pl.BlockSpec(memory_space=pltpu.SMEM)
HBM = pl.BlockSpec(memory_space=pltpu.HBM)
ANY = pl.BlockSpec(memory_space=pl.ANY)


def dot(a, b):
    return jnp.dot(a, b, preferred_element_type=F32)


def params(mib):
    return pltpu.CompilerParams(vmem_limit_bytes=mib * MIB)


def in_hbm(array):
    return pltpu.with_memory_space_constraint(array, pltpu.HBM)


def cost(flops, moved):
    return pl.CostEstimate(flops=flops, bytes_accessed=moved, transcendentals=0)


def in_vmem(array):
    return pltpu.with_memory_space_constraint(array, pltpu.VMEM)


def start(*copies):
    for copy in copies:
        copy.start()


def wait(*copies):
    for copy in copies:
        copy.wait()


def tiles(rows, count):
    return [pl.ds(i * (rows // count), rows // count) for i in range(count)]


def fetches(source, target, sems):
    parts = tiles(source.shape[0], sems.shape[0])
    copies = [
        pltpu.make_async_copy(source.at[part], target.at[part], sems.at[i])
        for i, part in enumerate(parts)
    ]
    return list(zip(parts, copies))


def weigh_kernel(members, me_ref, x_hbm, coef_hbm, *rest):
    outs, (x16, x32, coef, coef_sem, in_sems) = rest[:-5], rest[-5:]
    lats = coef.shape[0]
    coef_copy = pltpu.make_async_copy(coef_hbm, coef, coef_sem)
    coef_copy.start()
    block = lats * members
    parts = []
    for j in range(len(outs)):
        rows = pl.ds(pl.multiple_of((me_ref[0] ^ PARTNERS[j]) * block, block), block)
        parts.append(pltpu.make_async_copy(x_hbm.at[rows], x16.at[j], in_sems.at[j]))
    start(*parts)
    coef_copy.wait()
    for j, copy in enumerate(parts):
        copy.wait()
        slot = j % 2
        x32[slot, :block] = x16[j].astype(F32)
        for m in range(members):
            part = x32[slot, pl.ds(m, lats, stride=members), :]
            outs[j][:, m * LANES : (m + 1) * LANES] = (part * coef[...]).astype(BF16)


def weigh(me, field, coef):
    orders, lats, groups, parts, _ = field.shape
    members = groups * parts
    block = lats * members
    return pl.pallas_call(
        functools.partial(weigh_kernel, members),
        out_shape=[jax.ShapeDtypeStruct((lats, members * LANES), BF16)] * orders,
        in_specs=[SMEM, HBM, HBM],
        out_specs=[VMEM] * orders,
        scratch_shapes=[
            pltpu.VMEM((orders, block, LANES), BF16),
            pltpu.VMEM((2, block + SUBLANES, LANES), F32),
            pltpu.VMEM(coef.shape, F32),
            pltpu.SemaphoreType.DMA,
            pltpu.SemaphoreType.DMA((orders,)),
        ],
        compiler_params=params(12),
        cost_estimate=cost(field.size, field.size * 4),
    )(me, in_hbm(field.reshape(orders * block, LANES)), in_hbm(coef))


def analyse_kernel(me_ref, table_ref, *rest):
    blocks, (out_ref, w) = rest[:-2], rest[-2:]
    lats = blocks[0].shape[0]
    for j, block in enumerate(blocks):
        w[pl.ds(pl.multiple_of((me_ref[0] ^ PARTNERS[j]) * lats, lats), lats), :] = block[...]
    for rows in tiles(table_ref.shape[0], 4):
        out_ref[rows, :] = dot(table_ref[rows, :], w[...]).astype(BF16)


def analyse(me, table, blocks):
    rows, lats = table.shape
    columns = blocks[0].shape[1]
    return pl.pallas_call(
        analyse_kernel,
        out_shape=jax.ShapeDtypeStruct((rows, columns), BF16),
        in_specs=[SMEM] + [VMEM] * (1 + len(blocks)),
        out_specs=VMEM,
        scratch_shapes=[pltpu.VMEM((lats, columns), BF16)],
        compiler_params=params(14),
        cost_estimate=cost(2 * rows * lats * columns, 2 * rows * lats),
    )(me, table, *blocks)


def place_kernel(order_ref, table_hbm, owner_hbm, placed_ref, table, owner, chosen, table_sem, owner_sem):
    owner_copy = pltpu.make_async_copy(owner_hbm, owner, owner_sem)
    table_copy = pltpu.make_async_copy(table_hbm, table, table_sem)
    start(owner_copy, table_copy)
    degrees = table.shape[0]
    order = order_ref[0]
    owner_copy.wait()
    across = jnp.broadcast_to(owner[...], (LANES, degrees)).T
    for block in range(degrees // LANES):
        part = slice(block * LANES, (block + 1) * LANES)
        degree = lax.broadcasted_iota(jnp.int32, (degrees, LANES), 1) + block * LANES
        chosen[:, part] = ((across == degree) & (degree >= order)).astype(F32).astype(BF16)
    table_copy.wait()
    for rows in tiles(degrees, 4):
        placed_ref[rows, :] = dot(chosen[rows, :], table[...]).astype(BF16)


def place(order_ids, table, degree_owner):
    degrees, lats = table.shape
    return pl.pallas_call(
        place_kernel,
        out_shape=jax.ShapeDtypeStruct((degrees, lats), BF16),
        in_specs=[SMEM, HBM, HBM],
        out_specs=VMEM,
        scratch_shapes=[
            pltpu.VMEM(table.shape, BF16),
            pltpu.VMEM((1, degrees), jnp.int32),
            pltpu.VMEM((degrees, degrees), BF16),
            pltpu.SemaphoreType.DMA,
            pltpu.SemaphoreType.DMA,
        ],
        compiler_params=params(16),
        cost_estimate=cost(2 * degrees * degrees * lats, 4 * table.size),
    )(order_ids, in_hbm(table), in_hbm(degree_owner.reshape(1, degrees)))


def turn_kernel(table_ref, inv_hbm, turned_hbm, here_ref, turned, ring, sems, ring_sems):
    degrees, slots = here_ref.shape[0], ring.shape[0]

    def fetch(degree):
        slot = degree % slots
        return pltpu.make_async_copy(inv_hbm.at[degree], ring.at[slot], ring_sems.at[slot])

    for degree in range(slots):
        fetch(degree).start()
    copies = []
    for i, rows in enumerate(tiles(turned.shape[0], 4)):
        turned[rows, :] = table_ref[:, rows.start : rows.start + rows.size].T
        copies.append(pltpu.make_async_copy(turned.at[rows], turned_hbm.at[rows], sems.at[i]))
        copies[-1].start()
    for degree in range(degrees):
        fetch(degree).wait()
        here_ref[degree] = ring[degree % slots].T
        if degree + slots < degrees:
            fetch(degree + slots).start()
    wait(*copies)


def turn(table, inverses, count):
    turned = table.shape[::-1]
    radii = inverses.shape[1:]
    return pl.pallas_call(
        turn_kernel,
        out_shape=[pltpu.HBM(turned, BF16), pltpu.VMEM((count, *radii), BF16)],
        in_specs=[VMEM, HBM],
        out_specs=[HBM, VMEM],
        scratch_shapes=[
            pltpu.VMEM(turned, BF16),
            pltpu.VMEM((RING, *radii), BF16),
            pltpu.SemaphoreType.DMA((4,)),
            pltpu.SemaphoreType.DMA((RING,)),
        ],
        compiler_params=params(16),
        cost_estimate=cost(table.size, 4 * table.size + 4 * inverses.size),
    )(table, in_hbm(inverses))


def solve_kernel(orders, shards, members, x_ref, here_ref, inv_hbm, y_ref, x32, y32, inv, sems):
    degrees, held = inv_hbm.shape[0], here_ref.shape[0]
    parts = fetches(inv_hbm.at[held:], inv, sems)
    start(*[copy for _, copy in parts])
    each = (degrees - held) // len(parts)
    block = shards * degrees
    stride = block + 1
    half = degrees // 2

    def widen(part):
        for k in range(orders):
            for r in range(shards):
                first = r * degrees + part * half
                rows, to = pl.ds(k * block + first, half), pl.ds(k * stride + first, half)
                for m in range(members):
                    x32[m, to, :] = x_ref[rows, m * LANES : (m + 1) * LANES].astype(F32)

    def narrow(part):
        for k in range(orders):
            for r in range(shards):
                first = r * degrees + part * half
                rows, at = pl.ds(k * block + first, half), pl.ds(k * stride + first, half)
                for m in range(members):
                    y_ref[rows, m * LANES : (m + 1) * LANES] = y32[m, at, :].astype(BF16)

    def apply(degree):
        def rows(shard):
            return pl.ds(shard * degrees + degree, orders, stride=stride)

        x = jnp.concatenate(
            [
                jnp.concatenate([x32[m, rows(r), :] for r in range(shards)], axis=1)
                for m in range(members)
            ],
            axis=0,
        ).astype(BF16)
        if degree < held:
            y = dot(x, here_ref[degree])
        else:
            if (degree - held) % each == 0:
                parts[(degree - held) // each][1].wait()
            y = lax.dot_general(
                x, inv[degree - held], (((1,), (1,)), ((), ())), preferred_element_type=F32
            )
        for m in range(members):
            for r in range(shards):
                y32[m, rows(r), :] = y[m * orders : (m + 1) * orders, r * LANES : (r + 1) * LANES]

    for part in range(2):
        widen(part)
        for degree in range(part * half, (part + 1) * half):
            apply(degree)
        narrow(part)


def solve(owned, here, inverses, orders, shards, members):
    rows, columns = owned.shape
    degrees, radii, _ = inverses.shape
    rest = degrees - here.shape[0]
    return pl.pallas_call(
        functools.partial(solve_kernel, orders, shards, members),
        out_shape=jax.ShapeDtypeStruct((rows, columns), BF16),
        in_specs=[VMEM, VMEM, HBM],
        out_specs=VMEM,
        scratch_shapes=[pltpu.VMEM((members, rows + 2 * orders + rows // orders, LANES), F32)] * 2
        + [pltpu.VMEM((rest, radii, radii), BF16), pltpu.SemaphoreType.DMA((rest // 4,))],
        compiler_params=params(24),
        cost_estimate=cost(2 * degrees * radii * radii * orders * members, inverses.size),
    )(owned, in_vmem(here), in_hbm(inverses))


def synthesise_kernel(partners, me_ref, turned_ref, coeffs_ref, *outs):
    lats = outs[0].shape[0]
    for j, out in zip(partners, outs):
        rows = pl.ds(pl.multiple_of((me_ref[0] ^ j) * lats, lats), lats)
        out[...] = dot(turned_ref[rows, :], coeffs_ref[...]).astype(BF16)


def synthesise(me, turned, coeffs, partners):
    lats, degrees = turned.shape
    columns = coeffs.shape[1]
    count = len(partners)
    return pl.pallas_call(
        functools.partial(synthesise_kernel, partners),
        out_shape=[jax.ShapeDtypeStruct((lats // len(PARTNERS), columns), BF16)] * count,
        in_specs=[SMEM] + [VMEM] * 2,
        out_specs=[VMEM] * count,
        compiler_params=params(12),
        cost_estimate=cost(2 * degrees * lats * columns // 2, 2 * degrees * lats),
    )(me, turned, coeffs)


def assemble_kernel(members, me_ref, *rest):
    blocks, (out_hbm, y32, y16, out_sems) = rest[:-4], rest[-4:]
    lats = blocks[0].shape[0]
    block = lats * members
    copies = []
    for j, x_ref in enumerate(blocks):
        slot = j % 2
        for m in range(members):
            part = x_ref[:, m * LANES : (m + 1) * LANES].astype(F32)
            y32[slot, pl.ds(m, lats, stride=members), :] = part
        y16[j] = y32[slot, :block].astype(BF16)
        rows = pl.ds(pl.multiple_of((me_ref[0] ^ PARTNERS[j]) * block, block), block)
        copies.append(pltpu.make_async_copy(y16.at[j], out_hbm.at[rows], out_sems.at[j]))
        copies[-1].start()
    wait(*copies)


def assemble(me, received, shape):
    orders, lats, groups, parts, _ = shape
    members = groups * parts
    block = lats * members
    out = pl.pallas_call(
        functools.partial(assemble_kernel, members),
        out_shape=pltpu.HBM((orders * block, LANES), BF16),
        in_specs=[SMEM] + [VMEM] * orders,
        out_specs=HBM,
        scratch_shapes=[
            pltpu.VMEM((2, block + SUBLANES, LANES), F32),
            pltpu.VMEM((orders, block, LANES), BF16),
            pltpu.SemaphoreType.DMA((orders,)),
        ],
        compiler_params=params(12),
        cost_estimate=cost(orders * block * LANES, orders * block * LANES * 4),
    )(me, *received)
    return out.reshape(shape)


def exchange_rows(blocks, partners):
    n = lax.axis_size("row")
    return [
        block if not j else lax.ppermute(block, "row", [(a, a ^ j) for a in range(n)])
        for block, j in zip(blocks, partners)
    ]


def exchange_degrees(blocks):
    return lax.all_to_all(blocks, ("row", "col"), split_axis=0, concat_axis=0, tiled=True)


def tiled(field, coef, table, order_ids, inverses, degree_owner):
    n_row = lax.axis_size("row")
    n_col = lax.axis_size("col")
    orders, lats_dev, groups, parts, radii_dev = field.shape
    degrees_all, lats = table.shape[1:]
    deg_dev = inverses.shape[0]
    members = groups * parts
    columns = members * radii_dev

    me = lax.axis_index("row").astype(jnp.int32).reshape(1)

    weighted = list(weigh(me, field, coef))
    placed = place(order_ids, table[0], degree_owner)
    placed, *weighted[LATE:] = lax.optimization_barrier((placed, *weighted[LATE:]))
    arrived = exchange_rows(weighted, PARTNERS)
    turned, here = turn(placed, inverses, HELD)
    here, turned, arrived[0] = lax.optimization_barrier((here, turned, arrived[0]))
    spectral = analyse(me, placed, arrived)
    owned = exchange_degrees(spectral.reshape(n_row * n_col, deg_dev, columns))
    solved = solve(owned.reshape(degrees_all, columns), here, inverses, orders, n_col, members)
    coeffs = exchange_degrees(solved.reshape(n_row * n_col, deg_dev, columns))
    coeffs = coeffs.reshape(degrees_all, columns)
    outputs = synthesise(me, turned, coeffs, PARTNERS[:FIRST])
    received = exchange_rows(outputs, PARTNERS[:FIRST])
    if FIRST < len(PARTNERS):
        quick = 1
        received[quick], coeffs = lax.optimization_barrier((received[quick], coeffs))
        outputs = synthesise(me, turned, coeffs, PARTNERS[FIRST:])
        received += exchange_rows(outputs, PARTNERS[FIRST:])
    return assemble(me, received, field.shape)


def general(field, coef, table, order_ids, inverses, degree_owner):
    both = ("row", "col")
    n_row = lax.axis_size("row")
    n_col = lax.axis_size("col")
    orders, latitudes_dev = field.shape[:2]
    members = field.shape[2] * field.shape[3]
    radii_dev = field.shape[4]
    columns = members * radii_dev
    ord_dev, degrees_all, latitudes = table.shape
    deg_dev, radii, _ = inverses.shape
    devices = n_row * n_col

    weighted = (field.astype(F32) * coef[None, :, None, None, :]).astype(BF16)
    weighted = weighted.reshape(n_row, ord_dev, latitudes_dev, columns)
    arrived = lax.all_to_all(weighted, "row", split_axis=0, concat_axis=0, tiled=True)
    arrived = arrived.swapaxes(0, 1).reshape(ord_dev, latitudes, columns)

    degrees = lax.iota(jnp.int32, degrees_all)
    chosen = (degree_owner[:, None] == degrees[None, :])[None] & (
        degrees[None, None, :] >= order_ids[:, None, None]
    )
    placed_table = jnp.einsum(
        "kpl,klt->kpt", chosen.astype(BF16), table, preferred_element_type=F32
    ).astype(BF16)
    spectral = jnp.einsum(
        "kpt,ktn->kpn", placed_table, arrived, preferred_element_type=F32
    ).astype(BF16)
    spectral = spectral.reshape(ord_dev, devices, deg_dev, columns).swapaxes(0, 1)
    owned = lax.all_to_all(spectral, both, split_axis=0, concat_axis=0, tiled=True)
    owned = owned.reshape(n_row, n_col, ord_dev, deg_dev, members, radii_dev).swapaxes(1, 2)
    owned = owned.reshape(orders, n_col, deg_dev, members, radii_dev)
    solved = jnp.einsum(
        "kadms,dtas->kdmt",
        owned,
        inverses.reshape(deg_dev, radii, n_col, radii_dev),
        preferred_element_type=F32,
    ).astype(BF16)
    solved = solved.reshape(n_row, ord_dev, deg_dev, members, n_col, radii_dev)
    solved = solved.transpose(0, 4, 1, 2, 3, 5).reshape(devices, ord_dev, deg_dev, columns)
    coeffs = lax.all_to_all(solved, both, split_axis=0, concat_axis=0, tiled=True)
    coeffs = coeffs.swapaxes(0, 1).reshape(ord_dev, degrees_all, columns)
    outputs = jnp.einsum(
        "kpt,kpn->ktn", placed_table, coeffs, preferred_element_type=F32
    ).astype(BF16)
    outputs = outputs.reshape(ord_dev, n_row, latitudes_dev, columns).swapaxes(0, 1)
    outputs = lax.all_to_all(outputs, "row", split_axis=0, concat_axis=0, tiled=True)
    return outputs.reshape(field.shape)


def per_device(field, coef, table, order_ids, inverses, degree_owner):
    orders, lats, _, _, radii_dev = field.shape
    n_row = lax.axis_size("row")
    fits = (
        orders == n_row == SUBLANES
        and radii_dev == LANES
        and lats % 16 == 0
        and inverses.shape[0] % 16 == 0
        and table.shape[1] % 256 == 0
    )
    form = tiled if fits else general
    return form(field, coef, table, order_ids, inverses, degree_owner)


def solution(mesh):
    in_specs = (
        P(None, "row", None, None, "col"),
        P("row", "col"),
        P("row", None, None),
        P("row"),
        P(("row", "col"), None, None),
        P(),
    )
    out_specs = P(None, "row", None, None, "col")
    return jax.shard_map(
        per_device, mesh=mesh, in_specs=in_specs, out_specs=out_specs, check_vma=False
    )
```

```python
import functools

import jax
import jax.numpy as jnp
from jax import lax
from jax.experimental import pallas as pl
from jax.experimental.pallas import tpu as pltpu
from jax.sharding import PartitionSpec as P

LANES = 128
SUBLANES = 8
HELD = 32
GROUP = 4
FETCHED = 14
BESIDE = 0
FIRST = 5
LATE = 6
PARTNERS = (0, 6, 2, 4, 7, 1, 3, 5)
MIB = 1024 * 1024
BF16 = jnp.bfloat16
F32 = jnp.float32
VMEM = pl.BlockSpec(memory_space=pltpu.VMEM)
SMEM = pl.BlockSpec(memory_space=pltpu.SMEM)
HBM = pl.BlockSpec(memory_space=pltpu.HBM)
ANY = pl.BlockSpec(memory_space=pl.ANY)


def dot(a, b):
    return jnp.dot(a, b, preferred_element_type=F32)


def params(mib):
    return pltpu.CompilerParams(vmem_limit_bytes=mib * MIB)


def in_hbm(array):
    return pltpu.with_memory_space_constraint(array, pltpu.HBM)


def cost(flops, moved):
    return pl.CostEstimate(flops=flops, bytes_accessed=moved, transcendentals=0)


def in_vmem(array):
    return pltpu.with_memory_space_constraint(array, pltpu.VMEM)


def start(*copies):
    for copy in copies:
        copy.start()


def wait(*copies):
    for copy in copies:
        copy.wait()


def tiles(rows, count):
    return [pl.ds(i * (rows // count), rows // count) for i in range(count)]


def fetches(source, target, sems):
    parts = tiles(source.shape[0], sems.shape[0])
    copies = [
        pltpu.make_async_copy(source.at[part], target.at[part], sems.at[i])
        for i, part in enumerate(parts)
    ]
    return list(zip(parts, copies))


def weigh_kernel(members, me_ref, x_hbm, coef_hbm, *rest):
    outs, (x16, x32, coef, coef_sem, in_sems) = rest[:-5], rest[-5:]
    lats = coef.shape[0]
    coef_copy = pltpu.make_async_copy(coef_hbm, coef, coef_sem)
    coef_copy.start()
    block = lats * members
    parts = []
    for j in range(len(outs)):
        rows = pl.ds(pl.multiple_of((me_ref[0] ^ PARTNERS[j]) * block, block), block)
        parts.append(pltpu.make_async_copy(x_hbm.at[rows], x16.at[j], in_sems.at[j]))
    start(*parts)
    coef_copy.wait()
    for j, copy in enumerate(parts):
        copy.wait()
        slot = j % 2
        x32[slot, :block] = x16[j].astype(F32)
        for m in range(members):
            part = x32[slot, pl.ds(m, lats, stride=members), :]
            outs[j][:, m * LANES : (m + 1) * LANES] = (part * coef[...]).astype(BF16)


def weigh(me, field, coef):
    orders, lats, groups, parts, _ = field.shape
    members = groups * parts
    block = lats * members
    return pl.pallas_call(
        functools.partial(weigh_kernel, members),
        out_shape=[jax.ShapeDtypeStruct((lats, members * LANES), BF16)] * orders,
        in_specs=[SMEM, HBM, HBM],
        out_specs=[VMEM] * orders,
        scratch_shapes=[
            pltpu.VMEM((orders, block, LANES), BF16),
            pltpu.VMEM((2, block + SUBLANES, LANES), F32),
            pltpu.VMEM(coef.shape, F32),
            pltpu.SemaphoreType.DMA,
            pltpu.SemaphoreType.DMA((orders,)),
        ],
        compiler_params=params(12),
        cost_estimate=cost(field.size, field.size * 4),
    )(me, in_hbm(field.reshape(orders * block, LANES)), in_hbm(coef))


def analyse_kernel(me_ref, table_ref, *rest):
    blocks, (out_ref, w) = rest[:-2], rest[-2:]
    lats = blocks[0].shape[0]
    for j, block in enumerate(blocks):
        w[pl.ds(pl.multiple_of((me_ref[0] ^ PARTNERS[j]) * lats, lats), lats), :] = block[...]
    for rows in tiles(table_ref.shape[0], 4):
        out_ref[rows, :] = dot(table_ref[rows, :], w[...]).astype(BF16)


def analyse(me, table, blocks):
    rows, lats = table.shape
    columns = blocks[0].shape[1]
    return pl.pallas_call(
        analyse_kernel,
        out_shape=jax.ShapeDtypeStruct((rows, columns), BF16),
        in_specs=[SMEM] + [VMEM] * (1 + len(blocks)),
        out_specs=VMEM,
        scratch_shapes=[pltpu.VMEM((lats, columns), BF16)],
        compiler_params=params(14),
        cost_estimate=cost(2 * rows * lats * columns, 2 * rows * lats),
    )(me, table, *blocks)


def place_kernel(order_ref, table_hbm, owner_hbm, inv_hbm, placed_ref, raw_ref, *scratch):
    table, owner, chosen, table_sem, owner_sem, raw_sem = scratch
    owner_copy = pltpu.make_async_copy(owner_hbm, owner, owner_sem)
    table_copy = pltpu.make_async_copy(table_hbm, table, table_sem)
    raw_copy = pltpu.make_async_copy(inv_hbm.at[: raw_ref.shape[0]], raw_ref, raw_sem)
    start(owner_copy, table_copy, raw_copy)
    degrees = table.shape[0]
    order = order_ref[0]
    owner_copy.wait()
    across = jnp.broadcast_to(owner[...], (LANES, degrees)).T
    for block in range(degrees // LANES):
        part = slice(block * LANES, (block + 1) * LANES)
        degree = lax.broadcasted_iota(jnp.int32, (degrees, LANES), 1) + block * LANES
        chosen[:, part] = ((across == degree) & (degree >= order)).astype(F32).astype(BF16)
    table_copy.wait()
    for rows in tiles(degrees, 4):
        placed_ref[rows, :] = dot(chosen[rows, :], table[...]).astype(BF16)
    raw_copy.wait()


def place(order_ids, table, degree_owner, inverses, count):
    degrees, lats = table.shape
    return pl.pallas_call(
        place_kernel,
        out_shape=[
            jax.ShapeDtypeStruct((degrees, lats), BF16),
            pltpu.VMEM((count, *inverses.shape[1:]), BF16),
        ],
        in_specs=[SMEM, HBM, HBM, HBM],
        out_specs=[VMEM, VMEM],
        scratch_shapes=[
            pltpu.VMEM(table.shape, BF16),
            pltpu.VMEM((1, degrees), jnp.int32),
            pltpu.VMEM((degrees, degrees), BF16),
            pltpu.SemaphoreType.DMA,
            pltpu.SemaphoreType.DMA,
            pltpu.SemaphoreType.DMA,
        ],
        compiler_params=params(16),
        cost_estimate=cost(2 * degrees * degrees * lats, 4 * table.size),
    )(order_ids, in_hbm(table), in_hbm(degree_owner.reshape(1, degrees)), in_hbm(inverses))


def transpose_by_product(target, source, unit):
    size = unit.shape[0]
    for i in range(0, source.shape[1], size):
        for j in range(0, source.shape[0], size):
            target[i : i + size, j : j + size] = lax.dot_general(
                unit,
                source[j : j + size, i : i + size],
                (((1,), (1,)), ((), ())),
                preferred_element_type=F32,
            ).astype(BF16)


def turn_kernel(table_ref, raw_ref, inv_hbm, turned_hbm, here_ref, turned, ring, sems, ring_sems):
    ready, degrees = raw_ref.shape[0], here_ref.shape[0]
    fetched = [
        pltpu.make_async_copy(inv_hbm.at[ready + i], ring.at[i], ring_sems.at[i])
        for i in range(degrees - ready)
    ]
    start(*fetched)
    size = 2 * LANES
    place = lax.broadcasted_iota(jnp.int32, (size, size), 0)
    unit = (place == lax.broadcasted_iota(jnp.int32, (size, size), 1)).astype(F32).astype(BF16)
    copies = []
    table_parts = tiles(turned.shape[0], 4)
    each = BESIDE // len(table_parts)
    for i, rows in enumerate(table_parts):
        for degree in range(i * each, (i + 1) * each):
            transpose_by_product(here_ref.at[degree], raw_ref.at[degree], unit)
        turned[rows, :] = table_ref[:, rows.start : rows.start + rows.size].T
        copies.append(pltpu.make_async_copy(turned.at[rows], turned_hbm.at[rows], sems.at[i]))
        copies[-1].start()
    for first in range(BESIDE, degrees, GROUP):
        group = range(first, min(first + GROUP, degrees))
        wait(*[fetched[degree - ready] for degree in group if degree >= ready])
        for degree in group:
            source = raw_ref.at[degree] if degree < ready else ring.at[degree - ready]
            if degree % 2:
                transpose_by_product(here_ref.at[degree], source, unit)
            else:
                here_ref[degree] = source[...].T
    wait(*copies)


def turn(table, raw, inverses, count):
    turned = table.shape[::-1]
    radii = inverses.shape[1:]
    ring = count - raw.shape[0]
    return pl.pallas_call(
        turn_kernel,
        out_shape=[pltpu.HBM(turned, BF16), pltpu.VMEM((count, *radii), BF16)],
        in_specs=[VMEM, VMEM, HBM],
        out_specs=[HBM, VMEM],
        scratch_shapes=[
            pltpu.VMEM(turned, BF16),
            pltpu.VMEM((ring, *radii), BF16),
            pltpu.SemaphoreType.DMA((4,)),
            pltpu.SemaphoreType.DMA((ring,)),
        ],
        compiler_params=params(16),
        cost_estimate=cost(table.size, 4 * table.size + 4 * inverses.size),
    )(table, in_vmem(raw), in_hbm(inverses))


def solve_kernel(orders, shards, members, x_ref, here_ref, inv_hbm, y_ref, x32, y32, inv, sems):
    degrees, held = inv_hbm.shape[0], here_ref.shape[0]
    parts = fetches(inv_hbm.at[held:], inv, sems) if held < degrees else []
    start(*[copy for _, copy in parts])
    each = (degrees - held) // max(len(parts), 1)
    block = shards * degrees
    stride = block + 1
    half = degrees // 2

    def widen(part):
        for k in range(orders):
            for r in range(shards):
                first = r * degrees + part * half
                rows, to = pl.ds(k * block + first, half), pl.ds(k * stride + first, half)
                for m in range(members):
                    x32[m, to, :] = x_ref[rows, m * LANES : (m + 1) * LANES].astype(F32)

    def narrow(part):
        for k in range(orders):
            for r in range(shards):
                first = r * degrees + part * half
                rows, at = pl.ds(k * block + first, half), pl.ds(k * stride + first, half)
                for m in range(members):
                    y_ref[rows, m * LANES : (m + 1) * LANES] = y32[m, at, :].astype(BF16)

    def apply(degree):
        def rows(shard):
            return pl.ds(shard * degrees + degree, orders, stride=stride)

        x = jnp.concatenate(
            [
                jnp.concatenate([x32[m, rows(r), :] for r in range(shards)], axis=1)
                for m in range(members)
            ],
            axis=0,
        ).astype(BF16)
        if degree < held:
            y = dot(x, here_ref[degree])
        else:
            if (degree - held) % each == 0:
                parts[(degree - held) // each][1].wait()
            y = lax.dot_general(
                x, inv[degree - held], (((1,), (1,)), ((), ())), preferred_element_type=F32
            )
        for m in range(members):
            for r in range(shards):
                y32[m, rows(r), :] = y[m * orders : (m + 1) * orders, r * LANES : (r + 1) * LANES]

    for part in range(2):
        widen(part)
        for degree in range(part * half, (part + 1) * half):
            apply(degree)
        narrow(part)


def solve(owned, here, inverses, orders, shards, members):
    rows, columns = owned.shape
    degrees, radii, _ = inverses.shape
    rest = max(degrees - here.shape[0], 4)
    return pl.pallas_call(
        functools.partial(solve_kernel, orders, shards, members),
        out_shape=jax.ShapeDtypeStruct((rows, columns), BF16),
        in_specs=[VMEM, VMEM, HBM],
        out_specs=VMEM,
        scratch_shapes=[pltpu.VMEM((members, rows + 2 * orders + rows // orders, LANES), F32)] * 2
        + [pltpu.VMEM((rest, radii, radii), BF16), pltpu.SemaphoreType.DMA((rest // 4,))],
        compiler_params=params(24),
        cost_estimate=cost(2 * degrees * radii * radii * orders * members, inverses.size),
    )(owned, in_vmem(here), in_hbm(inverses))


def synthesise_kernel(partners, me_ref, turned_ref, coeffs_ref, *outs):
    lats = outs[0].shape[0]
    for j, out in zip(partners, outs):
        rows = pl.ds(pl.multiple_of((me_ref[0] ^ j) * lats, lats), lats)
        out[...] = dot(turned_ref[rows, :], coeffs_ref[...]).astype(BF16)


def synthesise(me, turned, coeffs, partners):
    lats, degrees = turned.shape
    columns = coeffs.shape[1]
    count = len(partners)
    return pl.pallas_call(
        functools.partial(synthesise_kernel, partners),
        out_shape=[jax.ShapeDtypeStruct((lats // len(PARTNERS), columns), BF16)] * count,
        in_specs=[SMEM] + [VMEM] * 2,
        out_specs=[VMEM] * count,
        compiler_params=params(12),
        cost_estimate=cost(2 * degrees * lats * columns // 2, 2 * degrees * lats),
    )(me, turned, coeffs)


def assemble_kernel(members, me_ref, *rest):
    blocks, (out_hbm, y32, y16, out_sems) = rest[:-4], rest[-4:]
    lats = blocks[0].shape[0]
    block = lats * members
    copies = []
    for j, x_ref in enumerate(blocks):
        slot = j % 2
        for m in range(members):
            part = x_ref[:, m * LANES : (m + 1) * LANES].astype(F32)
            y32[slot, pl.ds(m, lats, stride=members), :] = part
        y16[j] = y32[slot, :block].astype(BF16)
        rows = pl.ds(pl.multiple_of((me_ref[0] ^ PARTNERS[j]) * block, block), block)
        copies.append(pltpu.make_async_copy(y16.at[j], out_hbm.at[rows], out_sems.at[j]))
        copies[-1].start()
    wait(*copies)


def assemble(me, received, shape):
    orders, lats, groups, parts, _ = shape
    members = groups * parts
    block = lats * members
    out = pl.pallas_call(
        functools.partial(assemble_kernel, members),
        out_shape=pltpu.HBM((orders * block, LANES), BF16),
        in_specs=[SMEM] + [VMEM] * orders,
        out_specs=HBM,
        scratch_shapes=[
            pltpu.VMEM((2, block + SUBLANES, LANES), F32),
            pltpu.VMEM((orders, block, LANES), BF16),
            pltpu.SemaphoreType.DMA((orders,)),
        ],
        compiler_params=params(12),
        cost_estimate=cost(orders * block * LANES, orders * block * LANES * 4),
    )(me, *received)
    return out.reshape(shape)


def exchange_rows(blocks, partners):
    n = lax.axis_size("row")
    return [
        block if not j else lax.ppermute(block, "row", [(a, a ^ j) for a in range(n)])
        for block, j in zip(blocks, partners)
    ]


def exchange_degrees(blocks):
    return lax.all_to_all(blocks, ("row", "col"), split_axis=0, concat_axis=0, tiled=True)


def tiled(field, coef, table, order_ids, inverses, degree_owner):
    n_row = lax.axis_size("row")
    n_col = lax.axis_size("col")
    orders, lats_dev, groups, parts, radii_dev = field.shape
    degrees_all, lats = table.shape[1:]
    deg_dev = inverses.shape[0]
    members = groups * parts
    columns = members * radii_dev

    me = lax.axis_index("row").astype(jnp.int32).reshape(1)

    weighted = list(weigh(me, field, coef))
    placed, raw = place(order_ids, table[0], degree_owner, inverses, FETCHED)
    placed, *weighted[LATE:] = lax.optimization_barrier((placed, *weighted[LATE:]))
    arrived = exchange_rows(weighted, PARTNERS)
    turned, here = turn(placed, raw, inverses, HELD)
    here, turned, arrived[0] = lax.optimization_barrier((here, turned, arrived[0]))
    spectral = analyse(me, placed, arrived)
    owned = exchange_degrees(spectral.reshape(n_row * n_col, deg_dev, columns))
    solved = solve(owned.reshape(degrees_all, columns), here, inverses, orders, n_col, members)
    coeffs = exchange_degrees(solved.reshape(n_row * n_col, deg_dev, columns))
    coeffs = coeffs.reshape(degrees_all, columns)
    early, late = PARTNERS[1:FIRST], PARTNERS[:1] + PARTNERS[FIRST:]
    received = exchange_rows(synthesise(me, turned, coeffs, early), early)
    received[0], coeffs = lax.optimization_barrier((received[0], coeffs))
    own, *rest = exchange_rows(synthesise(me, turned, coeffs, late), late)
    return assemble(me, [own, *received, *rest], field.shape)


def general(field, coef, table, order_ids, inverses, degree_owner):
    both = ("row", "col")
    n_row = lax.axis_size("row")
    n_col = lax.axis_size("col")
    orders, latitudes_dev = field.shape[:2]
    members = field.shape[2] * field.shape[3]
    radii_dev = field.shape[4]
    columns = members * radii_dev
    ord_dev, degrees_all, latitudes = table.shape
    deg_dev, radii, _ = inverses.shape
    devices = n_row * n_col

    weighted = (field.astype(F32) * coef[None, :, None, None, :]).astype(BF16)
    weighted = weighted.reshape(n_row, ord_dev, latitudes_dev, columns)
    arrived = lax.all_to_all(weighted, "row", split_axis=0, concat_axis=0, tiled=True)
    arrived = arrived.swapaxes(0, 1).reshape(ord_dev, latitudes, columns)

    degrees = lax.iota(jnp.int32, degrees_all)
    chosen = (degree_owner[:, None] == degrees[None, :])[None] & (
        degrees[None, None, :] >= order_ids[:, None, None]
    )
    placed_table = jnp.einsum(
        "kpl,klt->kpt", chosen.astype(BF16), table, preferred_element_type=F32
    ).astype(BF16)
    spectral = jnp.einsum(
        "kpt,ktn->kpn", placed_table, arrived, preferred_element_type=F32
    ).astype(BF16)
    spectral = spectral.reshape(ord_dev, devices, deg_dev, columns).swapaxes(0, 1)
    owned = lax.all_to_all(spectral, both, split_axis=0, concat_axis=0, tiled=True)
    owned = owned.reshape(n_row, n_col, ord_dev, deg_dev, members, radii_dev).swapaxes(1, 2)
    owned = owned.reshape(orders, n_col, deg_dev, members, radii_dev)
    solved = jnp.einsum(
        "kadms,dtas->kdmt",
        owned,
        inverses.reshape(deg_dev, radii, n_col, radii_dev),
        preferred_element_type=F32,
    ).astype(BF16)
    solved = solved.reshape(n_row, ord_dev, deg_dev, members, n_col, radii_dev)
    solved = solved.transpose(0, 4, 1, 2, 3, 5).reshape(devices, ord_dev, deg_dev, columns)
    coeffs = lax.all_to_all(solved, both, split_axis=0, concat_axis=0, tiled=True)
    coeffs = coeffs.swapaxes(0, 1).reshape(ord_dev, degrees_all, columns)
    outputs = jnp.einsum(
        "kpt,kpn->ktn", placed_table, coeffs, preferred_element_type=F32
    ).astype(BF16)
    outputs = outputs.reshape(ord_dev, n_row, latitudes_dev, columns).swapaxes(0, 1)
    outputs = lax.all_to_all(outputs, "row", split_axis=0, concat_axis=0, tiled=True)
    return outputs.reshape(field.shape)


def per_device(field, coef, table, order_ids, inverses, degree_owner):
    orders, lats, _, _, radii_dev = field.shape
    n_row = lax.axis_size("row")
    fits = (
        orders == n_row == len(PARTNERS) == SUBLANES
        and inverses.shape[0] >= HELD
        and inverses.shape[1] % (2 * LANES) == 0
        and radii_dev == LANES
        and lats % 16 == 0
        and inverses.shape[0] % 16 == 0
        and table.shape[1] % 256 == 0
    )
    form = tiled if fits else general
    return form(field, coef, table, order_ids, inverses, degree_owner)


def solution(mesh):
    in_specs = (
        P(None, "row", None, None, "col"),
        P("row", "col"),
        P("row", None, None),
        P("row"),
        P(("row", "col"), None, None),
        P(),
    )
    out_specs = P(None, "row", None, None, "col")
    return jax.shard_map(
        per_device, mesh=mesh, in_specs=in_specs, out_specs=out_specs, check_vma=False
    )
```

```python
import functools

import jax
import jax.numpy as jnp
from jax import lax
from jax.experimental import pallas as pl
from jax.experimental.pallas import tpu as pltpu
from jax.sharding import PartitionSpec as P

LANES = 128
SUBLANES = 8
HELD = 28
GROUP = 4
FETCHED = 16
BESIDE = 0
FIRST = 5
LATE = 6
PARTNERS = (0, 6, 2, 4, 7, 1, 3, 5)
MIB = 1024 * 1024
BF16 = jnp.bfloat16
F32 = jnp.float32
VMEM = pl.BlockSpec(memory_space=pltpu.VMEM)
SMEM = pl.BlockSpec(memory_space=pltpu.SMEM)
HBM = pl.BlockSpec(memory_space=pltpu.HBM)
ANY = pl.BlockSpec(memory_space=pl.ANY)


def dot(a, b):
    return jnp.dot(a, b, preferred_element_type=F32)


def params(mib):
    return pltpu.CompilerParams(vmem_limit_bytes=mib * MIB)


def in_hbm(array):
    return pltpu.with_memory_space_constraint(array, pltpu.HBM)


def cost(flops, moved):
    return pl.CostEstimate(flops=flops, bytes_accessed=moved, transcendentals=0)


def in_vmem(array):
    return pltpu.with_memory_space_constraint(array, pltpu.VMEM)


def start(*copies):
    for copy in copies:
        copy.start()


def wait(*copies):
    for copy in copies:
        copy.wait()


def tiles(rows, count):
    return [pl.ds(i * (rows // count), rows // count) for i in range(count)]


def fetches(source, target, sems):
    parts = tiles(source.shape[0], sems.shape[0])
    copies = [
        pltpu.make_async_copy(source.at[part], target.at[part], sems.at[i])
        for i, part in enumerate(parts)
    ]
    return list(zip(parts, copies))


def weigh_kernel(members, me_ref, x_hbm, coef_hbm, *rest):
    outs, (x16, x32, coef, coef_sem, in_sems) = rest[:-5], rest[-5:]
    lats = coef.shape[0]
    coef_copy = pltpu.make_async_copy(coef_hbm, coef, coef_sem)
    coef_copy.start()
    block = lats * members
    parts = []
    for j in range(len(outs)):
        rows = pl.ds(pl.multiple_of((me_ref[0] ^ PARTNERS[j]) * block, block), block)
        parts.append(pltpu.make_async_copy(x_hbm.at[rows], x16.at[j], in_sems.at[j]))
    start(*parts)
    coef_copy.wait()
    for j, copy in enumerate(parts):
        copy.wait()
        slot = j % 2
        x32[slot, :block] = x16[j].astype(F32)
        for m in range(members):
            part = x32[slot, pl.ds(m, lats, stride=members), :]
            outs[j][:, m * LANES : (m + 1) * LANES] = (part * coef[...]).astype(BF16)


def weigh(me, field, coef):
    orders, lats, groups, parts, _ = field.shape
    members = groups * parts
    block = lats * members
    return pl.pallas_call(
        functools.partial(weigh_kernel, members),
        out_shape=[jax.ShapeDtypeStruct((lats, members * LANES), BF16)] * orders,
        in_specs=[SMEM, HBM, HBM],
        out_specs=[VMEM] * orders,
        scratch_shapes=[
            pltpu.VMEM((orders, block, LANES), BF16),
            pltpu.VMEM((2, block + SUBLANES, LANES), F32),
            pltpu.VMEM(coef.shape, F32),
            pltpu.SemaphoreType.DMA,
            pltpu.SemaphoreType.DMA((orders,)),
        ],
        compiler_params=params(12),
        cost_estimate=cost(field.size, field.size * 4),
    )(me, in_hbm(field.reshape(orders * block, LANES)), in_hbm(coef))


def analyse_kernel(me_ref, table_ref, *rest):
    blocks, (out_ref, w) = rest[:-2], rest[-2:]
    lats = blocks[0].shape[0]

    def rows(j):
        return pl.ds(pl.multiple_of((me_ref[0] ^ j) * lats, lats), lats)

    for j, block in zip(PARTNERS, blocks):
        w[rows(j), :] = block[...]
    for j in PARTNERS[len(blocks) :]:
        w[rows(j), :] = jnp.zeros(blocks[0].shape, BF16)
    for part in tiles(table_ref.shape[0], 4):
        out_ref[part, :] = dot(table_ref[part, :], w[...])


def analyse(me, table, blocks):
    rows, lats = table.shape
    columns = blocks[0].shape[1]
    return pl.pallas_call(
        analyse_kernel,
        out_shape=jax.ShapeDtypeStruct((rows, columns), F32),
        in_specs=[SMEM] + [VMEM] * (1 + len(blocks)),
        out_specs=VMEM,
        scratch_shapes=[pltpu.VMEM((lats, columns), BF16)],
        compiler_params=params(14),
        cost_estimate=cost(2 * rows * lats * columns, 2 * rows * lats),
    )(me, table, *blocks)


def add_rest_kernel(partners, me_ref, table_ref, sums_ref, *refs):
    blocks, (out_ref, w) = refs[:-2], refs[-2:]
    lats = blocks[0].shape[0]
    windows = []
    for i, (j, block) in enumerate(zip(partners, blocks)):
        at = me_ref[0] ^ j
        w[i] = jnp.zeros(w.shape[1:], BF16)
        w[i, pl.ds(pl.multiple_of(at % 2 * lats, lats), lats), :] = block[...]
        windows.append(pl.ds(pl.multiple_of(at // 2 * (2 * lats), 2 * lats), 2 * lats))
    for part in tiles(table_ref.shape[0], 4):
        total = sums_ref[part, :]
        for i, window in enumerate(windows):
            total = total + dot(table_ref[part, window], w[i])
        out_ref[part, :] = total.astype(BF16)


def add_rest(me, table, sums, blocks):
    rows, columns = sums.shape
    lats = blocks[0].shape[0]
    count = len(blocks)
    return pl.pallas_call(
        functools.partial(add_rest_kernel, PARTNERS[-count:]),
        out_shape=jax.ShapeDtypeStruct((rows, columns), BF16),
        in_specs=[SMEM] + [VMEM] * (2 + count),
        out_specs=VMEM,
        scratch_shapes=[pltpu.VMEM((count, 2 * lats, columns), BF16)],
        compiler_params=params(14),
        cost_estimate=cost(4 * rows * lats * columns * count, 4 * rows * lats * count),
    )(me, table, sums, *blocks)


def place_kernel(order_ref, table_hbm, owner_hbm, inv_hbm, placed_ref, raw_ref, *scratch):
    table, owner, chosen, table_sem, owner_sem, raw_sem = scratch
    owner_copy = pltpu.make_async_copy(owner_hbm, owner, owner_sem)
    table_copy = pltpu.make_async_copy(table_hbm, table, table_sem)
    raw_copy = pltpu.make_async_copy(inv_hbm.at[: raw_ref.shape[0]], raw_ref, raw_sem)
    start(owner_copy, table_copy, raw_copy)
    degrees = table.shape[0]
    order = order_ref[0]
    owner_copy.wait()
    across = jnp.broadcast_to(owner[...], (LANES, degrees)).T
    for block in range(degrees // LANES):
        part = slice(block * LANES, (block + 1) * LANES)
        degree = lax.broadcasted_iota(jnp.int32, (degrees, LANES), 1) + block * LANES
        chosen[:, part] = ((across == degree) & (degree >= order)).astype(F32).astype(BF16)
    table_copy.wait()
    for rows in tiles(degrees, 4):
        placed_ref[rows, :] = dot(chosen[rows, :], table[...]).astype(BF16)
    raw_copy.wait()


def place(order_ids, table, degree_owner, inverses, count):
    degrees, lats = table.shape
    return pl.pallas_call(
        place_kernel,
        out_shape=[
            jax.ShapeDtypeStruct((degrees, lats), BF16),
            pltpu.VMEM((count, *inverses.shape[1:]), BF16),
        ],
        in_specs=[SMEM, HBM, HBM, HBM],
        out_specs=[VMEM, VMEM],
        scratch_shapes=[
            pltpu.VMEM(table.shape, BF16),
            pltpu.VMEM((1, degrees), jnp.int32),
            pltpu.VMEM((degrees, degrees), BF16),
            pltpu.SemaphoreType.DMA,
            pltpu.SemaphoreType.DMA,
            pltpu.SemaphoreType.DMA,
        ],
        compiler_params=params(16),
        cost_estimate=cost(2 * degrees * degrees * lats, 4 * table.size),
    )(order_ids, in_hbm(table), in_hbm(degree_owner.reshape(1, degrees)), in_hbm(inverses))


def transpose_by_product(target, source, unit):
    size = unit.shape[0]
    for i in range(0, source.shape[1], size):
        for j in range(0, source.shape[0], size):
            target[i : i + size, j : j + size] = lax.dot_general(
                unit,
                source[j : j + size, i : i + size],
                (((1,), (1,)), ((), ())),
                preferred_element_type=F32,
            ).astype(BF16)


def turn_kernel(table_ref, raw_ref, inv_hbm, turned_hbm, here_ref, turned, ring, sems, ring_sems):
    ready, degrees = raw_ref.shape[0], here_ref.shape[0]
    fetched = [
        pltpu.make_async_copy(inv_hbm.at[ready + i], ring.at[i], ring_sems.at[i])
        for i in range(degrees - ready)
    ]
    start(*fetched)
    size = 2 * LANES
    place = lax.broadcasted_iota(jnp.int32, (size, size), 0)
    unit = (place == lax.broadcasted_iota(jnp.int32, (size, size), 1)).astype(F32).astype(BF16)
    copies = []
    table_parts = tiles(turned.shape[0], 4)
    each = BESIDE // len(table_parts)
    for i, rows in enumerate(table_parts):
        for degree in range(i * each, (i + 1) * each):
            transpose_by_product(here_ref.at[degree], raw_ref.at[degree], unit)
        turned[rows, :] = table_ref[:, rows.start : rows.start + rows.size].T
        copies.append(pltpu.make_async_copy(turned.at[rows], turned_hbm.at[rows], sems.at[i]))
        copies[-1].start()
    for first in range(BESIDE, degrees, GROUP):
        group = range(first, min(first + GROUP, degrees))
        wait(*[fetched[degree - ready] for degree in group if degree >= ready])
        for degree in group:
            source = raw_ref.at[degree] if degree < ready else ring.at[degree - ready]
            if degree % 2:
                transpose_by_product(here_ref.at[degree], source, unit)
            else:
                here_ref[degree] = source[...].T
    wait(*copies)


def turn(table, raw, inverses, count):
    turned = table.shape[::-1]
    radii = inverses.shape[1:]
    ring = count - raw.shape[0]
    return pl.pallas_call(
        turn_kernel,
        out_shape=[pltpu.HBM(turned, BF16), pltpu.VMEM((count, *radii), BF16)],
        in_specs=[VMEM, VMEM, HBM],
        out_specs=[HBM, VMEM],
        scratch_shapes=[
            pltpu.VMEM(turned, BF16),
            pltpu.VMEM((ring, *radii), BF16),
            pltpu.SemaphoreType.DMA((4,)),
            pltpu.SemaphoreType.DMA((ring,)),
        ],
        compiler_params=params(16),
        cost_estimate=cost(table.size, 4 * table.size + 4 * inverses.size),
    )(table, in_vmem(raw), in_hbm(inverses))


def solve_kernel(orders, shards, members, x_ref, here_ref, inv_hbm, y_ref, x32, y32, inv, sems):
    degrees, held = inv_hbm.shape[0], here_ref.shape[0]
    parts = fetches(inv_hbm.at[held:], inv, sems) if held < degrees else []
    start(*[copy for _, copy in parts])
    each = (degrees - held) // max(len(parts), 1)
    block = shards * degrees
    stride = block + 1
    half = degrees // 2

    def widen(part):
        for k in range(orders):
            for r in range(shards):
                first = r * degrees + part * half
                rows, to = pl.ds(k * block + first, half), pl.ds(k * stride + first, half)
                for m in range(members):
                    x32[m, to, :] = x_ref[rows, m * LANES : (m + 1) * LANES].astype(F32)

    def narrow(part):
        for k in range(orders):
            for r in range(shards):
                first = r * degrees + part * half
                rows, at = pl.ds(k * block + first, half), pl.ds(k * stride + first, half)
                for m in range(members):
                    y_ref[rows, m * LANES : (m + 1) * LANES] = y32[m, at, :].astype(BF16)

    def apply(degree):
        def rows(shard):
            return pl.ds(shard * degrees + degree, orders, stride=stride)

        x = jnp.concatenate(
            [
                jnp.concatenate([x32[m, rows(r), :] for r in range(shards)], axis=1)
                for m in range(members)
            ],
            axis=0,
        ).astype(BF16)
        if degree < held:
            y = dot(x, here_ref[degree])
        else:
            if (degree - held) % each == 0:
                parts[(degree - held) // each][1].wait()
            y = lax.dot_general(
                x, inv[degree - held], (((1,), (1,)), ((), ())), preferred_element_type=F32
            )
        for m in range(members):
            for r in range(shards):
                y32[m, rows(r), :] = y[m * orders : (m + 1) * orders, r * LANES : (r + 1) * LANES]

    for part in range(2):
        widen(part)
        for degree in range(part * half, (part + 1) * half):
            apply(degree)
        narrow(part)


def solve(owned, here, inverses, orders, shards, members):
    rows, columns = owned.shape
    degrees, radii, _ = inverses.shape
    rest = max(degrees - here.shape[0], 4)
    return pl.pallas_call(
        functools.partial(solve_kernel, orders, shards, members),
        out_shape=jax.ShapeDtypeStruct((rows, columns), BF16),
        in_specs=[VMEM, VMEM, HBM],
        out_specs=VMEM,
        scratch_shapes=[pltpu.VMEM((members, rows + 2 * orders + rows // orders, LANES), F32)] * 2
        + [pltpu.VMEM((rest, radii, radii), BF16), pltpu.SemaphoreType.DMA((rest // 4,))],
        compiler_params=params(24),
        cost_estimate=cost(2 * degrees * radii * radii * orders * members, inverses.size),
    )(owned, in_vmem(here), in_hbm(inverses))


def synthesise_kernel(partners, me_ref, turned_ref, coeffs_ref, *outs):
    lats = outs[0].shape[0]
    for j, out in zip(partners, outs):
        rows = pl.ds(pl.multiple_of((me_ref[0] ^ j) * lats, lats), lats)
        out[...] = dot(turned_ref[rows, :], coeffs_ref[...]).astype(BF16)


def synthesise(me, turned, coeffs, partners):
    lats, degrees = turned.shape
    columns = coeffs.shape[1]
    count = len(partners)
    return pl.pallas_call(
        functools.partial(synthesise_kernel, partners),
        out_shape=[jax.ShapeDtypeStruct((lats // len(PARTNERS), columns), BF16)] * count,
        in_specs=[SMEM] + [VMEM] * 2,
        out_specs=[VMEM] * count,
        compiler_params=params(12),
        cost_estimate=cost(2 * degrees * lats * columns // 2, 2 * degrees * lats),
    )(me, turned, coeffs)


def assemble_kernel(members, partners, me_ref, *rest):
    blocks, (out_hbm, y32, y16, out_sems) = rest[-4 - len(partners) : -4], rest[-4:]
    lats = blocks[0].shape[0]
    block = lats * members
    copies = []
    for i, (j, x_ref) in enumerate(zip(partners, blocks)):
        slot = i % 2
        for m in range(members):
            part = x_ref[:, m * LANES : (m + 1) * LANES].astype(F32)
            y32[slot, pl.ds(m, lats, stride=members), :] = part
        y16[i] = y32[slot, :block].astype(BF16)
        rows = pl.ds(pl.multiple_of((me_ref[0] ^ j) * block, block), block)
        copies.append(pltpu.make_async_copy(y16.at[i], out_hbm.at[rows], out_sems.at[i]))
        copies[-1].start()
    wait(*copies)


def assemble(me, received, partners, shape, so_far=None):
    orders, lats, groups, parts, _ = shape
    members = groups * parts
    block = lats * members
    count = len(partners)
    before = [] if so_far is None else [in_hbm(so_far)]
    return pl.pallas_call(
        functools.partial(assemble_kernel, members, partners),
        out_shape=pltpu.HBM((orders * block, LANES), BF16),
        in_specs=[SMEM] + [HBM] * len(before) + [VMEM] * count,
        out_specs=HBM,
        input_output_aliases={1: 0} if before else {},
        scratch_shapes=[
            pltpu.VMEM((2, block + SUBLANES, LANES), F32),
            pltpu.VMEM((count, block, LANES), BF16),
            pltpu.SemaphoreType.DMA((count,)),
        ],
        compiler_params=params(12),
        cost_estimate=cost(count * block * LANES, count * block * LANES * 4),
    )(me, *before, *received)


def exchange_rows(blocks, partners):
    n = lax.axis_size("row")
    return [
        block if not j else lax.ppermute(block, "row", [(a, a ^ j) for a in range(n)])
        for block, j in zip(blocks, partners)
    ]


def exchange_degrees(blocks):
    return lax.all_to_all(blocks, ("row", "col"), split_axis=0, concat_axis=0, tiled=True)


def tiled(field, coef, table, order_ids, inverses, degree_owner):
    n_row = lax.axis_size("row")
    n_col = lax.axis_size("col")
    orders, lats_dev, groups, parts, radii_dev = field.shape
    degrees_all, lats = table.shape[1:]
    deg_dev = inverses.shape[0]
    members = groups * parts
    columns = members * radii_dev

    me = lax.axis_index("row").astype(jnp.int32).reshape(1)

    weighted = list(weigh(me, field, coef))
    placed, raw = place(order_ids, table[0], degree_owner, inverses, FETCHED)
    placed, *weighted[LATE:] = lax.optimization_barrier((placed, *weighted[LATE:]))
    arrived = exchange_rows(weighted, PARTNERS)
    turned, here = turn(placed, raw, inverses, HELD)
    here, turned, arrived[0] = lax.optimization_barrier((here, turned, arrived[0]))
    sums = analyse(me, placed, arrived[:LATE])
    spectral = add_rest(me, placed, sums, arrived[LATE:])
    owned = exchange_degrees(spectral.reshape(n_row * n_col, deg_dev, columns))
    solved = solve(owned.reshape(degrees_all, columns), here, inverses, orders, n_col, members)
    coeffs = exchange_degrees(solved.reshape(n_row * n_col, deg_dev, columns))
    coeffs = coeffs.reshape(degrees_all, columns)
    early, late = PARTNERS[1:FIRST], PARTNERS[:1] + PARTNERS[FIRST:]
    received = exchange_rows(synthesise(me, turned, coeffs, early), early)
    received[0], coeffs = lax.optimization_barrier((received[0], coeffs))
    own, *rest = exchange_rows(synthesise(me, turned, coeffs, late), late)
    received = [own, *received, *rest]
    out = assemble(me, received[:LATE], PARTNERS[:LATE], field.shape)
    out = assemble(me, received[LATE:], PARTNERS[LATE:], field.shape, out)
    return out.reshape(field.shape)


def general(field, coef, table, order_ids, inverses, degree_owner):
    both = ("row", "col")
    n_row = lax.axis_size("row")
    n_col = lax.axis_size("col")
    orders, latitudes_dev = field.shape[:2]
    members = field.shape[2] * field.shape[3]
    radii_dev = field.shape[4]
    columns = members * radii_dev
    ord_dev, degrees_all, latitudes = table.shape
    deg_dev, radii, _ = inverses.shape
    devices = n_row * n_col

    weighted = (field.astype(F32) * coef[None, :, None, None, :]).astype(BF16)
    weighted = weighted.reshape(n_row, ord_dev, latitudes_dev, columns)
    arrived = lax.all_to_all(weighted, "row", split_axis=0, concat_axis=0, tiled=True)
    arrived = arrived.swapaxes(0, 1).reshape(ord_dev, latitudes, columns)

    degrees = lax.iota(jnp.int32, degrees_all)
    chosen = (degree_owner[:, None] == degrees[None, :])[None] & (
        degrees[None, None, :] >= order_ids[:, None, None]
    )
    placed_table = jnp.einsum(
        "kpl,klt->kpt", chosen.astype(BF16), table, preferred_element_type=F32
    ).astype(BF16)
    spectral = jnp.einsum(
        "kpt,ktn->kpn", placed_table, arrived, preferred_element_type=F32
    ).astype(BF16)
    spectral = spectral.reshape(ord_dev, devices, deg_dev, columns).swapaxes(0, 1)
    owned = lax.all_to_all(spectral, both, split_axis=0, concat_axis=0, tiled=True)
    owned = owned.reshape(n_row, n_col, ord_dev, deg_dev, members, radii_dev).swapaxes(1, 2)
    owned = owned.reshape(orders, n_col, deg_dev, members, radii_dev)
    solved = jnp.einsum(
        "kadms,dtas->kdmt",
        owned,
        inverses.reshape(deg_dev, radii, n_col, radii_dev),
        preferred_element_type=F32,
    ).astype(BF16)
    solved = solved.reshape(n_row, ord_dev, deg_dev, members, n_col, radii_dev)
    solved = solved.transpose(0, 4, 1, 2, 3, 5).reshape(devices, ord_dev, deg_dev, columns)
    coeffs = lax.all_to_all(solved, both, split_axis=0, concat_axis=0, tiled=True)
    coeffs = coeffs.swapaxes(0, 1).reshape(ord_dev, degrees_all, columns)
    outputs = jnp.einsum(
        "kpt,kpn->ktn", placed_table, coeffs, preferred_element_type=F32
    ).astype(BF16)
    outputs = outputs.reshape(ord_dev, n_row, latitudes_dev, columns).swapaxes(0, 1)
    outputs = lax.all_to_all(outputs, "row", split_axis=0, concat_axis=0, tiled=True)
    return outputs.reshape(field.shape)


def per_device(field, coef, table, order_ids, inverses, degree_owner):
    orders, lats, _, _, radii_dev = field.shape
    n_row = lax.axis_size("row")
    fits = (
        orders == n_row == len(PARTNERS) == SUBLANES
        and inverses.shape[0] >= HELD
        and inverses.shape[1] % (2 * LANES) == 0
        and radii_dev == LANES
        and lats % LANES in (0, LANES // 2)
        and inverses.shape[0] % 16 == 0
        and table.shape[1] % 256 == 0
    )
    form = tiled if fits else general
    return form(field, coef, table, order_ids, inverses, degree_owner)


def solution(mesh):
    in_specs = (
        P(None, "row", None, None, "col"),
        P("row", "col"),
        P("row", None, None),
        P("row"),
        P(("row", "col"), None, None),
        P(),
    )
    out_specs = P(None, "row", None, None, "col")
    return jax.shard_map(
        per_device, mesh=mesh, in_specs=in_specs, out_specs=out_specs, check_vma=False
    )
```

```python
import functools

import jax
import jax.numpy as jnp
from jax import lax
from jax.experimental import pallas as pl
from jax.experimental.pallas import tpu as pltpu
from jax.sharding import PartitionSpec as P

LANES = 128
SUBLANES = 8
HELD = 28
GROUP = 4
FETCHED = 16
BESIDE = 0
FIRST = 5
LATE = 6
PARTNERS = (0, 6, 7, 2, 4, 1, 3, 5)
MIB = 1024 * 1024
BF16 = jnp.bfloat16
F32 = jnp.float32
VMEM = pl.BlockSpec(memory_space=pltpu.VMEM)
SMEM = pl.BlockSpec(memory_space=pltpu.SMEM)
HBM = pl.BlockSpec(memory_space=pltpu.HBM)
ANY = pl.BlockSpec(memory_space=pl.ANY)


def dot(a, b):
    return jnp.dot(a, b, preferred_element_type=F32)


def params(mib):
    return pltpu.CompilerParams(vmem_limit_bytes=mib * MIB)


def in_hbm(array):
    return pltpu.with_memory_space_constraint(array, pltpu.HBM)


def cost(flops, moved):
    return pl.CostEstimate(flops=flops, bytes_accessed=moved, transcendentals=0)


def in_vmem(array):
    return pltpu.with_memory_space_constraint(array, pltpu.VMEM)


def start(*copies):
    for copy in copies:
        copy.start()


def wait(*copies):
    for copy in copies:
        copy.wait()


def tiles(rows, count):
    return [pl.ds(i * (rows // count), rows // count) for i in range(count)]


def fetches(source, target, sems):
    parts = tiles(source.shape[0], sems.shape[0])
    copies = [
        pltpu.make_async_copy(source.at[part], target.at[part], sems.at[i])
        for i, part in enumerate(parts)
    ]
    return list(zip(parts, copies))


def weigh_kernel(members, me_ref, x_hbm, coef_hbm, *rest):
    outs, (x16, x32, coef, coef_sem, in_sems) = rest[:-5], rest[-5:]
    lats = coef.shape[0]
    coef_copy = pltpu.make_async_copy(coef_hbm, coef, coef_sem)
    coef_copy.start()
    block = lats * members
    parts = []
    for j in range(len(outs)):
        rows = pl.ds(pl.multiple_of((me_ref[0] ^ PARTNERS[j]) * block, block), block)
        parts.append(pltpu.make_async_copy(x_hbm.at[rows], x16.at[j], in_sems.at[j]))
    start(*parts)
    coef_copy.wait()
    for j, copy in enumerate(parts):
        copy.wait()
        slot = j % 2
        x32[slot, :block] = x16[j].astype(F32)
        for m in range(members):
            part = x32[slot, pl.ds(m, lats, stride=members), :]
            outs[j][:, m * LANES : (m + 1) * LANES] = (part * coef[...]).astype(BF16)


def weigh(me, field, coef):
    orders, lats, groups, parts, _ = field.shape
    members = groups * parts
    block = lats * members
    return pl.pallas_call(
        functools.partial(weigh_kernel, members),
        out_shape=[jax.ShapeDtypeStruct((lats, members * LANES), BF16)] * orders,
        in_specs=[SMEM, HBM, HBM],
        out_specs=[VMEM] * orders,
        scratch_shapes=[
            pltpu.VMEM((orders, block, LANES), BF16),
            pltpu.VMEM((2, block + SUBLANES, LANES), F32),
            pltpu.VMEM(coef.shape, F32),
            pltpu.SemaphoreType.DMA,
            pltpu.SemaphoreType.DMA((orders,)),
        ],
        compiler_params=params(12),
        cost_estimate=cost(field.size, field.size * 4),
    )(me, in_hbm(field.reshape(orders * block, LANES)), in_hbm(coef))


def analyse_kernel(me_ref, table_ref, *rest):
    blocks, (out_ref, w) = rest[:-2], rest[-2:]
    lats = blocks[0].shape[0]

    def rows(j):
        return pl.ds(pl.multiple_of((me_ref[0] ^ j) * lats, lats), lats)

    for j, block in zip(PARTNERS, blocks):
        w[rows(j), :] = block[...]
    for j in PARTNERS[len(blocks) :]:
        w[rows(j), :] = jnp.zeros(blocks[0].shape, BF16)
    for part in tiles(table_ref.shape[0], 4):
        out_ref[part, :] = dot(table_ref[part, :], w[...])


def analyse(me, table, blocks):
    rows, lats = table.shape
    columns = blocks[0].shape[1]
    return pl.pallas_call(
        analyse_kernel,
        out_shape=jax.ShapeDtypeStruct((rows, columns), F32),
        in_specs=[SMEM] + [VMEM] * (1 + len(blocks)),
        out_specs=VMEM,
        scratch_shapes=[pltpu.VMEM((lats, columns), BF16)],
        compiler_params=params(14),
        cost_estimate=cost(2 * rows * lats * columns, 2 * rows * lats),
    )(me, table, *blocks)


def add_rest_kernel(partners, me_ref, table_ref, sums_ref, *refs):
    blocks, (out_ref, w) = refs[:-2], refs[-2:]
    lats = blocks[0].shape[0]
    windows = []
    for i, (j, block) in enumerate(zip(partners, blocks)):
        at = me_ref[0] ^ j
        w[i] = jnp.zeros(w.shape[1:], BF16)
        w[i, pl.ds(pl.multiple_of(at % 2 * lats, lats), lats), :] = block[...]
        windows.append(pl.ds(pl.multiple_of(at // 2 * (2 * lats), 2 * lats), 2 * lats))
    for part in tiles(table_ref.shape[0], 4):
        total = sums_ref[part, :]
        for i, window in enumerate(windows):
            total = total + dot(table_ref[part, window], w[i])
        out_ref[part, :] = total.astype(BF16)


def add_rest(me, table, sums, blocks):
    rows, columns = sums.shape
    lats = blocks[0].shape[0]
    count = len(blocks)
    return pl.pallas_call(
        functools.partial(add_rest_kernel, PARTNERS[-count:]),
        out_shape=jax.ShapeDtypeStruct((rows, columns), BF16),
        in_specs=[SMEM] + [VMEM] * (2 + count),
        out_specs=VMEM,
        scratch_shapes=[pltpu.VMEM((count, 2 * lats, columns), BF16)],
        compiler_params=params(14),
        cost_estimate=cost(4 * rows * lats * columns * count, 4 * rows * lats * count),
    )(me, table, sums, *blocks)


def place_kernel(order_ref, table_hbm, owner_hbm, inv_hbm, placed_ref, raw_ref, *scratch):
    table, owner, chosen, table_sem, owner_sem, raw_sem = scratch
    owner_copy = pltpu.make_async_copy(owner_hbm, owner, owner_sem)
    table_copy = pltpu.make_async_copy(table_hbm, table, table_sem)
    raw_copy = pltpu.make_async_copy(inv_hbm.at[: raw_ref.shape[0]], raw_ref, raw_sem)
    start(owner_copy, table_copy, raw_copy)
    degrees = table.shape[0]
    order = order_ref[0]
    owner_copy.wait()
    across = jnp.broadcast_to(owner[...], (LANES, degrees)).T
    for block in range(degrees // LANES):
        part = slice(block * LANES, (block + 1) * LANES)
        degree = lax.broadcasted_iota(jnp.int32, (degrees, LANES), 1) + block * LANES
        chosen[:, part] = ((across == degree) & (degree >= order)).astype(F32).astype(BF16)
    table_copy.wait()
    for rows in tiles(degrees, 4):
        placed_ref[rows, :] = dot(chosen[rows, :], table[...]).astype(BF16)
    raw_copy.wait()


def place(order_ids, table, degree_owner, inverses, count):
    degrees, lats = table.shape
    return pl.pallas_call(
        place_kernel,
        out_shape=[
            jax.ShapeDtypeStruct((degrees, lats), BF16),
            pltpu.VMEM((count, *inverses.shape[1:]), BF16),
        ],
        in_specs=[SMEM, HBM, HBM, HBM],
        out_specs=[VMEM, VMEM],
        scratch_shapes=[
            pltpu.VMEM(table.shape, BF16),
            pltpu.VMEM((1, degrees), jnp.int32),
            pltpu.VMEM((degrees, degrees), BF16),
            pltpu.SemaphoreType.DMA,
            pltpu.SemaphoreType.DMA,
            pltpu.SemaphoreType.DMA,
        ],
        compiler_params=params(16),
        cost_estimate=cost(2 * degrees * degrees * lats, 4 * table.size),
    )(order_ids, in_hbm(table), in_hbm(degree_owner.reshape(1, degrees)), in_hbm(inverses))


def transpose_by_product(target, source, unit):
    size = unit.shape[0]
    for i in range(0, source.shape[1], size):
        for j in range(0, source.shape[0], size):
            target[i : i + size, j : j + size] = lax.dot_general(
                unit,
                source[j : j + size, i : i + size],
                (((1,), (1,)), ((), ())),
                preferred_element_type=F32,
            ).astype(BF16)


def turn_kernel(table_ref, raw_ref, inv_hbm, turned_hbm, here_ref, turned, ring, sems, ring_sems):
    ready, degrees = raw_ref.shape[0], here_ref.shape[0]
    fetched = [
        pltpu.make_async_copy(inv_hbm.at[ready + i], ring.at[i], ring_sems.at[i])
        for i in range(degrees - ready)
    ]
    start(*fetched)
    size = 2 * LANES
    place = lax.broadcasted_iota(jnp.int32, (size, size), 0)
    unit = (place == lax.broadcasted_iota(jnp.int32, (size, size), 1)).astype(F32).astype(BF16)
    copies = []
    table_parts = tiles(turned.shape[0], 4)
    each = BESIDE // len(table_parts)
    for i, rows in enumerate(table_parts):
        for degree in range(i * each, (i + 1) * each):
            transpose_by_product(here_ref.at[degree], raw_ref.at[degree], unit)
        turned[rows, :] = table_ref[:, rows.start : rows.start + rows.size].T
        copies.append(pltpu.make_async_copy(turned.at[rows], turned_hbm.at[rows], sems.at[i]))
        copies[-1].start()
    for first in range(BESIDE, degrees, GROUP):
        group = range(first, min(first + GROUP, degrees))
        wait(*[fetched[degree - ready] for degree in group if degree >= ready])
        for degree in group:
            source = raw_ref.at[degree] if degree < ready else ring.at[degree - ready]
            if degree % 2:
                transpose_by_product(here_ref.at[degree], source, unit)
            else:
                here_ref[degree] = source[...].T
    wait(*copies)


def turn(table, raw, inverses, count):
    turned = table.shape[::-1]
    radii = inverses.shape[1:]
    ring = count - raw.shape[0]
    return pl.pallas_call(
        turn_kernel,
        out_shape=[pltpu.HBM(turned, BF16), pltpu.VMEM((count, *radii), BF16)],
        in_specs=[VMEM, VMEM, HBM],
        out_specs=[HBM, VMEM],
        scratch_shapes=[
            pltpu.VMEM(turned, BF16),
            pltpu.VMEM((ring, *radii), BF16),
            pltpu.SemaphoreType.DMA((4,)),
            pltpu.SemaphoreType.DMA((ring,)),
        ],
        compiler_params=params(16),
        cost_estimate=cost(table.size, 4 * table.size + 4 * inverses.size),
    )(table, in_vmem(raw), in_hbm(inverses))


def solve_kernel(orders, shards, members, x_ref, here_ref, inv_hbm, y_ref, x32, y32, inv, sems):
    degrees, held = inv_hbm.shape[0], here_ref.shape[0]
    parts = fetches(inv_hbm.at[held:], inv, sems) if held < degrees else []
    start(*[copy for _, copy in parts])
    each = (degrees - held) // max(len(parts), 1)
    block = shards * degrees
    stride = block + 1
    half = degrees // 2

    def widen(part):
        for k in range(orders):
            for r in range(shards):
                first = r * degrees + part * half
                rows, to = pl.ds(k * block + first, half), pl.ds(k * stride + first, half)
                for m in range(members):
                    x32[m, to, :] = x_ref[rows, m * LANES : (m + 1) * LANES].astype(F32)

    def narrow(part):
        for k in range(orders):
            for r in range(shards):
                first = r * degrees + part * half
                rows, at = pl.ds(k * block + first, half), pl.ds(k * stride + first, half)
                for m in range(members):
                    y_ref[rows, m * LANES : (m + 1) * LANES] = y32[m, at, :].astype(BF16)

    def apply(degree):
        def rows(shard):
            return pl.ds(shard * degrees + degree, orders, stride=stride)

        x = jnp.concatenate(
            [
                jnp.concatenate([x32[m, rows(r), :] for r in range(shards)], axis=1)
                for m in range(members)
            ],
            axis=0,
        ).astype(BF16)
        if degree < held:
            y = dot(x, here_ref[degree])
        else:
            if (degree - held) % each == 0:
                parts[(degree - held) // each][1].wait()
            y = lax.dot_general(
                x, inv[degree - held], (((1,), (1,)), ((), ())), preferred_element_type=F32
            )
        for m in range(members):
            for r in range(shards):
                y32[m, rows(r), :] = y[m * orders : (m + 1) * orders, r * LANES : (r + 1) * LANES]

    for part in range(2):
        widen(part)
        for degree in range(part * half, (part + 1) * half):
            apply(degree)
        narrow(part)


def solve(owned, here, inverses, orders, shards, members):
    rows, columns = owned.shape
    degrees, radii, _ = inverses.shape
    rest = max(degrees - here.shape[0], 4)
    return pl.pallas_call(
        functools.partial(solve_kernel, orders, shards, members),
        out_shape=jax.ShapeDtypeStruct((rows, columns), BF16),
        in_specs=[VMEM, VMEM, HBM],
        out_specs=VMEM,
        scratch_shapes=[pltpu.VMEM((members, rows + 2 * orders + rows // orders, LANES), F32)] * 2
        + [pltpu.VMEM((rest, radii, radii), BF16), pltpu.SemaphoreType.DMA((rest // 4,))],
        compiler_params=params(24),
        cost_estimate=cost(2 * degrees * radii * radii * orders * members, inverses.size),
    )(owned, in_vmem(here), in_hbm(inverses))


def synthesise_kernel(partners, me_ref, turned_ref, coeffs_ref, *outs):
    lats = outs[0].shape[0]
    for j, out in zip(partners, outs):
        rows = pl.ds(pl.multiple_of((me_ref[0] ^ j) * lats, lats), lats)
        out[...] = dot(turned_ref[rows, :], coeffs_ref[...]).astype(BF16)


def synthesise(me, turned, coeffs, partners):
    lats, degrees = turned.shape
    columns = coeffs.shape[1]
    count = len(partners)
    return pl.pallas_call(
        functools.partial(synthesise_kernel, partners),
        out_shape=[jax.ShapeDtypeStruct((lats // len(PARTNERS), columns), BF16)] * count,
        in_specs=[SMEM] + [VMEM] * 2,
        out_specs=[VMEM] * count,
        compiler_params=params(12),
        cost_estimate=cost(2 * degrees * lats * columns // 2, 2 * degrees * lats),
    )(me, turned, coeffs)


def assemble_kernel(members, partners, me_ref, *rest):
    blocks, (out_hbm, y32, y16, out_sems) = rest[-4 - len(partners) : -4], rest[-4:]
    lats = blocks[0].shape[0]
    block = lats * members
    copies = []
    for i, (j, x_ref) in enumerate(zip(partners, blocks)):
        slot = i % 2
        for m in range(members):
            part = x_ref[:, m * LANES : (m + 1) * LANES].astype(F32)
            y32[slot, pl.ds(m, lats, stride=members), :] = part
        y16[i] = y32[slot, :block].astype(BF16)
        rows = pl.ds(pl.multiple_of((me_ref[0] ^ j) * block, block), block)
        copies.append(pltpu.make_async_copy(y16.at[i], out_hbm.at[rows], out_sems.at[i]))
        copies[-1].start()
    wait(*copies)


def assemble(me, received, partners, shape, so_far=None):
    orders, lats, groups, parts, _ = shape
    members = groups * parts
    block = lats * members
    count = len(partners)
    before = [] if so_far is None else [in_hbm(so_far)]
    return pl.pallas_call(
        functools.partial(assemble_kernel, members, partners),
        out_shape=pltpu.HBM((orders * block, LANES), BF16),
        in_specs=[SMEM] + [HBM] * len(before) + [VMEM] * count,
        out_specs=HBM,
        input_output_aliases={1: 0} if before else {},
        scratch_shapes=[
            pltpu.VMEM((2, block + SUBLANES, LANES), F32),
            pltpu.VMEM((count, block, LANES), BF16),
            pltpu.SemaphoreType.DMA((count,)),
        ],
        compiler_params=params(12),
        cost_estimate=cost(count * block * LANES, count * block * LANES * 4),
    )(me, *before, *received)


def exchange_rows(blocks, partners):
    n = lax.axis_size("row")
    return [
        block if not j else lax.ppermute(block, "row", [(a, a ^ j) for a in range(n)])
        for block, j in zip(blocks, partners)
    ]


def exchange_degrees(blocks):
    return lax.all_to_all(blocks, ("row", "col"), split_axis=0, concat_axis=0, tiled=True)


def tiled(field, coef, table, order_ids, inverses, degree_owner):
    n_row = lax.axis_size("row")
    n_col = lax.axis_size("col")
    orders, lats_dev, groups, parts, radii_dev = field.shape
    degrees_all, lats = table.shape[1:]
    deg_dev = inverses.shape[0]
    members = groups * parts
    columns = members * radii_dev

    me = lax.axis_index("row").astype(jnp.int32).reshape(1)

    weighted = list(weigh(me, field, coef))
    placed, raw = place(order_ids, table[0], degree_owner, inverses, FETCHED)
    placed, *weighted[LATE:] = lax.optimization_barrier((placed, *weighted[LATE:]))
    arrived = exchange_rows(weighted, PARTNERS)
    turned, here = turn(placed, raw, inverses, HELD)
    here, turned, arrived[0] = lax.optimization_barrier((here, turned, arrived[0]))
    sums = analyse(me, placed, arrived[:LATE])
    spectral = add_rest(me, placed, sums, arrived[LATE:])
    owned = exchange_degrees(spectral.reshape(n_row * n_col, deg_dev, columns))
    solved = solve(owned.reshape(degrees_all, columns), here, inverses, orders, n_col, members)
    coeffs = exchange_degrees(solved.reshape(n_row * n_col, deg_dev, columns))
    coeffs = coeffs.reshape(degrees_all, columns)
    early, late = PARTNERS[1:FIRST], PARTNERS[:1] + PARTNERS[FIRST:]
    received = exchange_rows(synthesise(me, turned, coeffs, early), early)
    received[0], coeffs = lax.optimization_barrier((received[0], coeffs))
    own, *rest = exchange_rows(synthesise(me, turned, coeffs, late), late)
    received = [own, *received, *rest]
    out = assemble(me, received[:LATE], PARTNERS[:LATE], field.shape)
    out = assemble(me, received[LATE:], PARTNERS[LATE:], field.shape, out)
    return out.reshape(field.shape)


def general(field, coef, table, order_ids, inverses, degree_owner):
    both = ("row", "col")
    n_row = lax.axis_size("row")
    n_col = lax.axis_size("col")
    orders, latitudes_dev = field.shape[:2]
    members = field.shape[2] * field.shape[3]
    radii_dev = field.shape[4]
    columns = members * radii_dev
    ord_dev, degrees_all, latitudes = table.shape
    deg_dev, radii, _ = inverses.shape
    devices = n_row * n_col

    weighted = (field.astype(F32) * coef[None, :, None, None, :]).astype(BF16)
    weighted = weighted.reshape(n_row, ord_dev, latitudes_dev, columns)
    arrived = lax.all_to_all(weighted, "row", split_axis=0, concat_axis=0, tiled=True)
    arrived = arrived.swapaxes(0, 1).reshape(ord_dev, latitudes, columns)

    degrees = lax.iota(jnp.int32, degrees_all)
    chosen = (degree_owner[:, None] == degrees[None, :])[None] & (
        degrees[None, None, :] >= order_ids[:, None, None]
    )
    placed_table = jnp.einsum(
        "kpl,klt->kpt", chosen.astype(BF16), table, preferred_element_type=F32
    ).astype(BF16)
    spectral = jnp.einsum(
        "kpt,ktn->kpn", placed_table, arrived, preferred_element_type=F32
    ).astype(BF16)
    spectral = spectral.reshape(ord_dev, devices, deg_dev, columns).swapaxes(0, 1)
    owned = lax.all_to_all(spectral, both, split_axis=0, concat_axis=0, tiled=True)
    owned = owned.reshape(n_row, n_col, ord_dev, deg_dev, members, radii_dev).swapaxes(1, 2)
    owned = owned.reshape(orders, n_col, deg_dev, members, radii_dev)
    solved = jnp.einsum(
        "kadms,dtas->kdmt",
        owned,
        inverses.reshape(deg_dev, radii, n_col, radii_dev),
        preferred_element_type=F32,
    ).astype(BF16)
    solved = solved.reshape(n_row, ord_dev, deg_dev, members, n_col, radii_dev)
    solved = solved.transpose(0, 4, 1, 2, 3, 5).reshape(devices, ord_dev, deg_dev, columns)
    coeffs = lax.all_to_all(solved, both, split_axis=0, concat_axis=0, tiled=True)
    coeffs = coeffs.swapaxes(0, 1).reshape(ord_dev, degrees_all, columns)
    outputs = jnp.einsum(
        "kpt,kpn->ktn", placed_table, coeffs, preferred_element_type=F32
    ).astype(BF16)
    outputs = outputs.reshape(ord_dev, n_row, latitudes_dev, columns).swapaxes(0, 1)
    outputs = lax.all_to_all(outputs, "row", split_axis=0, concat_axis=0, tiled=True)
    return outputs.reshape(field.shape)


def per_device(field, coef, table, order_ids, inverses, degree_owner):
    orders, lats, _, _, radii_dev = field.shape
    n_row = lax.axis_size("row")
    fits = (
        orders == n_row == len(PARTNERS) == SUBLANES
        and inverses.shape[0] >= HELD
        and inverses.shape[1] % (2 * LANES) == 0
        and radii_dev == LANES
        and lats % LANES in (0, LANES // 2)
        and inverses.shape[0] % 16 == 0
        and table.shape[1] % 256 == 0
    )
    form = tiled if fits else general
    return form(field, coef, table, order_ids, inverses, degree_owner)


def solution(mesh):
    in_specs = (
        P(None, "row", None, None, "col"),
        P("row", "col"),
        P("row", None, None),
        P("row"),
        P(("row", "col"), None, None),
        P(),
    )
    out_specs = P(None, "row", None, None, "col")
    return jax.shard_map(
        per_device, mesh=mesh, in_specs=in_specs, out_specs=out_specs, check_vma=False
    )
```
